128 devices in a mesh: dp: 16 (over y, z_lo, core), section: 4 (over x), grp: 2 (over z_hi).
Axes of the slice: x: 4, y: 4, z: 4 (z_hi: 2, z_lo: 2; z = z_hi * 2 + z_lo), core: 2. Of those that a mesh axis runs over, the one named last changes fastest.
Arguments:
- enc_input: bfloat16 [2, 64, 48, 4096], P(None, ('dp', 'section')), may hold values from -20 to 20
- weights: bfloat16 [2, 4096, 1024], P('grp'), may hold values from -0.75 to 0.75
- enc_gain: float32 [4096], replicated, may hold values from 0.1 to 1.9
- enc_bias: float32 [1024], replicated, may hold values from -3 to 3
- mask_token: float32 [1024], replicated, may hold values from -6 to 6
- pos_embed: float32 [192, 1024], replicated, may hold values from -6 to 6
- dec_gains: float32 [2, 1024], replicated, may hold values from 0.1 to 1.9
- head_weight: bfloat16 [1024, 256], replicated, may hold values from -0.1875 to 0.1875
- head_bias: float32 [256], replicated, may hold values from -3 to 3
- order: int32 [2, 64, 192], P(None, ('dp', 'section')), may hold values from 0 to 191, each once within a row
- targets: bfloat16 [2, 64, 192, 256], P(None, ('dp', 'section')), may hold values from -6 to 6
Outputs:
- input_grads: bfloat16 [2, 2, 64, 48, 4096], P('grp', None, ('dp', 'section'))
- weight_grads: float32 [2, 4096, 1024], P('grp', ('dp', 'section'))
The draws below stay inside these ranges and needn't reach their ends.
Inputs may be any that keep to these rules, and one draw needn't show every extreme that they name: Each row of order lists every one of the 192 positions once; its first 48 entries are the visible tokens, in the order of the rows of enc_input.
All inputs are finite; a program needn't handle non-finite values.
Results may differ from the reference program's by a relative error of at most 0.015.
Values may be sent and summed in bfloat16 or wider, within the bound.
A program may use at most 192 MiB of HBM per device.

```python
import math
import jax
import jax.numpy as jnp
from jax import lax

D = 1024
DE = 4096
H = 16
HS = 64
PIX = 256
L = 192
MB = 2
VIS = 48
MASKED = 144
SAMPLES = 64


def draw_enc_input(key, part):
    key = jax.random.fold_in(key, 11)
    base_key, row_key = jax.random.split(key, 2)
    shape = (MB, SAMPLES, VIS, DE)
    rows = jnp.exp(jax.random.uniform(row_key, (MB, SAMPLES, VIS, 1), minval=math.log(0.5), maxval=math.log(5.0)))
    values = jax.random.normal(base_key, shape) * rows
    return jnp.clip(values, -20.0, 20.0).astype(jnp.bfloat16)


def draw_weights(key, part):
    key = jax.random.fold_in(key, 23)
    base_key = jax.random.fold_in(key, 0)
    base = jnp.clip(jax.random.normal(base_key, (2, DE, D)), -4.0, 4.0)
    encoder_slot = base[0] / math.sqrt(DE)
    decoder_slot = base[1] / math.sqrt(D)
    values = jnp.stack([encoder_slot, decoder_slot])
    return jnp.clip(values, -0.75, 0.75).astype(jnp.bfloat16)


def block_scale(own_key, extent, cuts, least, top_value):
    level = 1.0
    for axis_at, parts in cuts:
        draws = jax.random.uniform(jax.random.fold_in(jax.random.fold_in(own_key, 6), axis_at), (parts,), jnp.float32, least / len(cuts), top_value / len(cuts))
        level = level * jnp.repeat(jnp.exp(draws), extent[axis_at] // parts).reshape((-1,) + (1,) * (len(extent) - 1 - axis_at))
    return level


def noise(rng, dims, scale, limit, pieces=(), kind=jnp.bfloat16):
    array = scale * jax.random.normal(rng, dims, jnp.float32)
    if pieces:
        array = array * block_scale(rng, dims, pieces, -0.22, 0.18)
    return jnp.clip(array, -limit, limit).astype(kind)


def setup_inputs(seed: int = 0) -> dict:
    arg_keys = jax.random.split(jax.random.key(seed), 12)
    enc_input = draw_enc_input(jax.random.fold_in(arg_keys[11], 71), 0)
    weights = draw_weights(jax.random.fold_in(arg_keys[11], 71), 0)
    enc_gain = jnp.clip(1.0 + 0.18 * jax.random.normal(arg_keys[2], (DE,), jnp.float32), 0.1, 1.9)
    enc_bias = noise(arg_keys[3], (D,), 0.5, 3.0, (), jnp.float32)
    mask_token = noise(arg_keys[4], (D,), 1.0, 6.0, (), jnp.float32)
    pos_embed = noise(arg_keys[5], (L, D), 1.0, 6.0, (), jnp.float32)
    dec_gains = jnp.clip(1.0 + 0.18 * jax.random.normal(arg_keys[6], (2, D), jnp.float32), 0.1, 1.9)
    head_weight = noise(arg_keys[7], (D, PIX), D ** -0.5, 0.1875)
    head_bias = noise(arg_keys[8], (PIX,), 0.5, 3.0, (), jnp.float32)
    order = jax.vmap(lambda own: jax.random.permutation(own, L))(jax.random.split(arg_keys[9], MB * SAMPLES)).reshape((MB, SAMPLES, L)).astype(jnp.int32)
    targets = noise(arg_keys[10], (MB, SAMPLES, L, PIX), 1.0, 6.0, ((1, 64),))
    return {"enc_input": enc_input, "weights": weights, "enc_gain": enc_gain, "enc_bias": enc_bias, "mask_token": mask_token, "pos_embed": pos_embed, "dec_gains": dec_gains, "head_weight": head_weight, "head_bias": head_bias, "order": order, "targets": targets}


EPS = 1e-06

def norm_forward(values, gain):
    rstd = lax.rsqrt(lax.optimization_barrier(jnp.mean(values * values, axis=-1, keepdims=True)) + EPS)
    return (values * rstd * gain, rstd)

def norm_backward(values, rstd, gain, upstream):
    scaled = upstream * gain
    inner = lax.optimization_barrier(jnp.mean(scaled * values, axis=-1, keepdims=True))
    return rstd * scaled - values * (rstd * rstd * rstd) * inner

def as_float(values):
    return values.astype(jnp.float32)

def encode_sample(block, w_enc, enc_gain, enc_bias):
    normed, rstd = norm_forward(block.astype(jnp.float32), enc_gain)
    normed_b = normed.astype(jnp.bfloat16)
    latent = (jnp.dot(normed_b, w_enc, preferred_element_type=jnp.float32) + enc_bias).astype(jnp.bfloat16)
    return (latent, normed_b, rstd)

def decoder_sample(latent, positions, target_rows, w_dec, mask_token, pos_embed, dec_gains, head_weight, head_bias):
    fill = jnp.broadcast_to(mask_token, (MASKED, D))
    stream = jnp.concatenate([latent.astype(jnp.float32), fill], 0) + jnp.take(pos_embed, positions, axis=0)
    normed, rstd_in = norm_forward(stream, dec_gains[0])
    act = normed.astype(jnp.bfloat16)
    stacked = w_dec[:3 * D].reshape(3, D, D)
    w_out = w_dec[3 * D:]
    qkv = jnp.einsum('ti,gio->gto', as_float(act), as_float(stacked)).astype(jnp.bfloat16)
    heads_qkv = qkv.reshape(3, L, H, HS)
    query, keys, values = (heads_qkv[0], heads_qkv[1], heads_qkv[2])
    scale = 1.0 / math.sqrt(HS)
    scores = jnp.einsum('qhd,khd->hqk', as_float(query), as_float(keys)) * scale
    peak = lax.optimization_barrier(jnp.max(scores, axis=-1, keepdims=True))
    expo = jnp.exp(scores - peak)
    probs = expo / lax.optimization_barrier(jnp.sum(expo, axis=-1, keepdims=True))
    probs_b = probs.astype(jnp.bfloat16)
    attended = jnp.einsum('hqk,khd->qhd', as_float(probs_b), as_float(values)).reshape(L, D).astype(jnp.bfloat16)
    hidden = stream + jnp.dot(attended, w_out, preferred_element_type=jnp.float32)
    out_normed, rstd_out = norm_forward(hidden, dec_gains[1])
    out_b = out_normed.astype(jnp.bfloat16)
    pred = jnp.dot(out_b, head_weight, preferred_element_type=jnp.float32) + head_bias
    wanted = jnp.take(target_rows, positions, axis=0).astype(jnp.float32)
    error = (pred - wanted).astype(jnp.bfloat16)
    d_out = jnp.dot(error, head_weight.T, preferred_element_type=jnp.float32)
    d_hidden = norm_backward(hidden, rstd_out, dec_gains[1], d_out)
    d_hidden_b = d_hidden.astype(jnp.bfloat16)
    d_att = jnp.dot(d_hidden_b, w_out.T, preferred_element_type=jnp.float32).astype(jnp.bfloat16)
    d_att_h = d_att.reshape(L, H, HS)
    d_probs = jnp.einsum('qhd,khd->hqk', as_float(d_att_h), as_float(values))
    d_values = jnp.einsum('hqk,qhd->khd', as_float(probs_b), as_float(d_att_h)).astype(jnp.bfloat16)
    d_scores = (probs * (d_probs - lax.optimization_barrier(jnp.sum(d_probs * probs, axis=-1, keepdims=True))) * scale).astype(jnp.bfloat16)
    d_query = jnp.einsum('hqk,khd->qhd', as_float(d_scores), as_float(keys)).astype(jnp.bfloat16)
    d_keys = jnp.einsum('hqk,qhd->khd', as_float(d_scores), as_float(query)).astype(jnp.bfloat16)
    d_qkv = jnp.stack([d_query, d_keys, d_values]).reshape(3, L, D)
    d_act = jnp.einsum('gto,gio->ti', as_float(d_qkv), as_float(stacked))
    d_stream = d_hidden + norm_backward(stream, rstd_in, dec_gains[0], d_act)
    term_qkv = jnp.einsum('ti,gto->gio', as_float(act), as_float(d_qkv)).reshape(3 * D, D)
    term_out = jnp.dot(attended.T, d_hidden_b, preferred_element_type=jnp.float32)
    return (d_stream.astype(jnp.bfloat16), jnp.concatenate([term_qkv, term_out], 0))

def reference(enc_input, weights, enc_gain, enc_bias, mask_token, pos_embed, dec_gains, head_weight, head_bias, order, targets):
    w_enc = weights[0]
    w_dec = weights[1]
    count = MB * SAMPLES
    inputs = (enc_input.reshape(count, VIS, DE), order.reshape(count, L), targets.reshape(count, L, PIX))

    def per_sample(carry, items):
        block, positions, target_rows = items
        latent, normed_b, rstd = encode_sample(block, w_enc, enc_gain, enc_bias)
        d_stream_b, dec_term = decoder_sample(latent, positions, target_rows, w_dec, mask_token, pos_embed, dec_gains, head_weight, head_bias)
        d_latent = d_stream_b[:VIS]
        enc_term = jnp.dot(normed_b.T, d_latent, preferred_element_type=jnp.float32)
        d_normed = jnp.dot(d_latent, w_enc.T, preferred_element_type=jnp.float32)
        d_block = norm_backward(block.astype(jnp.float32), rstd, enc_gain, d_normed).astype(jnp.bfloat16)
        return ((carry[0] + enc_term, carry[1] + dec_term), (d_block, d_stream_b.reshape(VIS, DE)))
    zeros = jnp.zeros((DE, D), jnp.float32)
    sums, grads = lax.scan(per_sample, (zeros, zeros), inputs)
    input_grads = jnp.stack([grads[0].reshape(MB, SAMPLES, VIS, DE), grads[1].reshape(MB, SAMPLES, VIS, DE)])
    weight_grads = jnp.stack([sums[0], sums[1]]) / count
    return (input_grads, weight_grads)
```

```python
import functools
import math

import jax
import jax.numpy as jnp
from jax import lax
from jax.experimental import pallas as pl
from jax.experimental.pallas import tpu as pltpu
from jax.sharding import PartitionSpec as P

MESH = pl.DeviceIdType.MESH
B16 = jnp.bfloat16
F32 = jnp.float32


def rs_kernel(
    scale, p_ref, o_ref,
    acc_x, acc_y, core_x, core_y, r1_x, r1_y, r2_x, r2_y,
    acc2_x, acc2_y, s1_x, s1_y, s2_x, s2_y, zr,
    load_sem, core_send, core_recv, ssem, rsem, ssem2, rsem2, zsend, zrecv,
):
    dp = lax.axis_index("dp")
    x = lax.axis_index("section")
    y = dp // 4
    z = (dp // 2) % 2
    c = dp % 2

    def at_y(t):
        return {"dp": t * 4 + z * 2 + c}

    def at_x(t):
        return {"section": t}

    to_core = {"dp": y * 4 + z * 2 + (1 - c)}
    to_z = {"dp": y * 4 + (1 - z) * 2 + c}
    xs = [(x + 2) % 4, (x + 1) % 4, (x + 3) % 4, x]
    ys = [(y + 2) % 4, (y + 1) % 4, (y + 3) % 4, y]

    barrier = pltpu.get_barrier_semaphore()
    for who in (to_core, to_z, at_x(xs[1]), at_x(xs[2]), at_y(ys[1]), at_y(ys[2])):
        pl.semaphore_signal(barrier, inc=1, device_id=who, device_id_type=MESH)
    pl.semaphore_wait(barrier, 6)

    def remote(src, dst, send, recv, who):
        return pltpu.make_async_remote_copy(
            src_ref=src, dst_ref=dst, send_sem=send, recv_sem=recv,
            device_id=who, device_id_type=MESH,
        )

    def px(j, core):
        return p_ref.at[:, :, core, xs[j], pl.ds(0, 32)]

    def py(j, core):
        return p_ref.at[ys[j], :, core, :, pl.ds(32, 32)]

    order = [(0, 0), (1, 0), (0, 1), (0, 2), (1, 1), (1, 2), (0, 3), (1, 3)]
    loads, cores = {}, {}
    parts = (px, py)
    accs, corebufs = (acc_x, acc_y), (core_x, core_y)
    for a, j in order:
        cores[a, j] = remote(
            parts[a](j, 1 - c), corebufs[a].at[j], core_send.at[a, j], core_recv.at[a, j], to_core
        )
        cores[a, j].start()
        loads[a, j] = pltpu.make_async_copy(parts[a](j, c), accs[a].at[j], load_sem.at[a, j])
        loads[a, j].start()

    started = []

    def half(ref, h):
        n = ref.shape[0] // 2
        return ref.at[pl.ds(h * n, n)]

    def send(src, dst, send_s, recv_s, who):
        copy = remote(src, dst, send_s, recv_s, who)
        copy.start()
        started.append(copy)
        return copy

    def merge(a, j):
        cores[a, j].wait_recv()
        loads[a, j].wait()
        accs[a][j] = accs[a][j] + corebufs[a][j]

    def add_half(acc, j, h, got):
        n = acc.shape[1] // 2
        sl = pl.ds(h * n, n)
        acc[j, sl] = acc[j, sl] + got[...]

    class Axis:
        def __init__(self, acc, r1, r2, ss, rs, plus, minus):
            self.acc, self.r1, self.r2 = acc, r1, r2
            self.ss, self.rs, self.plus, self.minus = ss, rs, plus, minus

        def step1(self):
            a = self.acc
            self.c0 = send(half(a.at[0], 0), self.r1.at[0], self.ss.at[0], self.rs.at[0], self.plus)
            self.c1 = send(half(a.at[0], 1), self.r1.at[1], self.ss.at[1], self.rs.at[1], self.minus)

        def step2(self):
            a = self.acc
            self.c2 = send(half(a.at[1], 1), half(self.r2.at[0], 1), self.ss.at[2], self.rs.at[2], self.plus)
            self.c3 = send(half(a.at[2], 0), half(self.r2.at[1], 0), self.ss.at[3], self.rs.at[3], self.minus)

        def step3(self):
            a = self.acc
            self.c0.wait_recv()
            add_half(a, 1, 0, self.r1.at[0])
            self.c4 = send(half(a.at[1], 0), half(self.r2.at[0], 0), self.ss.at[4], self.rs.at[4], self.plus)
            self.c1.wait_recv()
            add_half(a, 2, 1, self.r1.at[1])
            self.c5 = send(half(a.at[2], 1), half(self.r2.at[1], 1), self.ss.at[5], self.rs.at[5], self.minus)

        def finish_waits(self):
            for copy in (self.c2, self.c3, self.c4, self.c5):
                copy.wait_recv()

    first = (
        Axis(acc_x, r1_x, r2_x, ssem.at[0], rsem.at[0], at_x(xs[1]), at_x(xs[2])),
        Axis(acc_y, r1_y, r2_y, ssem.at[1], rsem.at[1], at_y(ys[1]), at_y(ys[2])),
    )
    second = (
        Axis(acc2_x, s1_x, s2_x, ssem2.at[0], rsem2.at[0], at_y(ys[1]), at_y(ys[2])),
        Axis(acc2_y, s1_y, s2_y, ssem2.at[1], rsem2.at[1], at_x(xs[1]), at_x(xs[2])),
    )
    for a in (0, 1):
        merge(a, 0)
        first[a].step1()
    for a in (0, 1):
        merge(a, 1)
        merge(a, 2)
        first[a].step2()
    for a in (0, 1):
        first[a].step3()
    for a in (0, 1):
        merge(a, 3)

    def total(ax, a, j):
        r2 = ax.r2
        if a == 0:
            rows = lambda ref: ref[ys[j]]
        else:
            rows = lambda ref: ref[:, xs[j]]
        value = (
            rows(ax.acc.at[3]).astype(F32) + rows(r2.at[0]).astype(F32) + rows(r2.at[1]).astype(F32)
        )
        second[a].acc[j] = value.astype(B16)

    for a in (0, 1):
        first[a].finish_waits()
        total(first[a], a, 0)
        second[a].step1()
        total(first[a], a, 1)
        total(first[a], a, 2)
        second[a].step2()
        total(first[a], a, 3)
    for a in (0, 1):
        second[a].step3()
    zcopies = []
    for a in (0, 1):
        ax = second[a]
        ax.finish_waits()
        value = ax.acc[3].astype(F32) + ax.r2[0].astype(F32) + ax.r2[1].astype(F32)
        ax.acc[3] = value.astype(B16)
        zcopies.append(send(ax.acc.at[3, 1 - z], zr.at[a], zsend.at[a], zrecv.at[a], to_z))
    for a in (0, 1):
        zcopies[a].wait_recv()
        o_ref[pl.ds(a * 32, 32), :] = (
            second[a].acc[3, z].astype(F32) + zr[a].astype(F32)
        ) * scale
    for key in cores:
        cores[key].wait_send()
    for copy in started:
        copy.wait_send()


def reduce_scatter(part, scale):
    rows, width = part.shape
    p = part.reshape(4, 2, 2, 4, 64, width)
    V = pltpu.VMEM
    D = pltpu.SemaphoreType.DMA
    return pl.pallas_call(
        functools.partial(rs_kernel, scale),
        out_shape=jax.ShapeDtypeStruct((64, width), F32),
        in_specs=[pl.BlockSpec(memory_space=pl.ANY)],
        out_specs=pl.BlockSpec(memory_space=pltpu.VMEM),
        scratch_shapes=[
            V((4, 4, 2, 32, width), B16), V((4, 2, 4, 32, width), B16),
            V((4, 4, 2, 32, width), B16), V((4, 2, 4, 32, width), B16),
            V((2, 2, 2, 32, width), B16), V((2, 1, 4, 32, width), B16),
            V((2, 4, 2, 32, width), B16), V((2, 2, 4, 32, width), B16),
            V((4, 2, 32, width), B16), V((4, 2, 32, width), B16),
            V((2, 1, 32, width), B16), V((2, 1, 32, width), B16),
            V((2, 2, 32, width), B16), V((2, 2, 32, width), B16),
            V((2, 32, width), B16),
            D((2, 4)), D((2, 4)), D((2, 4)), D((2, 6)), D((2, 6)), D((2, 6)), D((2, 6)), D((2,)), D((2,)),
        ],
        compiler_params=pltpu.CompilerParams(
            collective_id=0, has_side_effects=True, vmem_limit_bytes=40 * 2**20
        ),
        name="reduce_scatter",
    )(p)


H = 16
HS = 64


EPS = 1e-06


def from_behind(block, axis, distance):
    devices = range(lax.axis_size(axis))
    route = [(i - distance, i) for i in devices if i - distance in devices]
    return lax.ppermute(block, axis, route)


def norm_forward(values, gain):
    rstd = lax.rsqrt(jnp.mean(values * values, axis=-1, keepdims=True) + EPS)
    return (values * rstd * gain, rstd)


def norm_backward(values, rstd, gain, upstream):
    scaled = upstream * gain
    inner = jnp.mean(scaled * values, axis=-1, keepdims=True)
    return rstd * scaled - values * (rstd * rstd * rstd) * inner


def encoder_forward(block, w_main, enc_gain, enc_bias):
    normed, rstd = norm_forward(block.astype(jnp.float32), enc_gain)
    normed_b = normed.astype(jnp.bfloat16)
    latent = (
        jnp.einsum("svc,cd->svd", normed_b, w_main, preferred_element_type=jnp.float32) + enc_bias
    )
    return (latent.astype(jnp.bfloat16), normed_b, rstd)


def encoder_backward(block, normed_b, rstd, w_main, enc_gain, d_latent, total):
    term = jnp.einsum("svc,svd->cd", normed_b, d_latent, preferred_element_type=jnp.float32)
    d_normed = jnp.einsum("svd,cd->svc", d_latent, w_main, preferred_element_type=jnp.float32)
    d_block = norm_backward(block.astype(jnp.float32), rstd, enc_gain, d_normed)
    return (d_block.astype(jnp.bfloat16), total + term)


def decoder_sample(latent, positions, target_rows, w_main, extras):
    mask_token, pos_embed, dec_gains, head_weight, head_bias = extras
    visible, width = latent.shape
    length = positions.shape[0]
    fill = jnp.broadcast_to(mask_token, (length - visible, width))
    stream = jnp.concatenate([latent.astype(jnp.float32), fill], 0) + jnp.take(
        pos_embed, positions, axis=0
    )
    normed, rstd_in = norm_forward(stream, dec_gains[0])
    act = normed.astype(jnp.bfloat16)
    stacked = w_main[: 3 * width].reshape(3, width, width)
    w_out = w_main[3 * width :]
    qkv = jnp.einsum("ti,gio->gto", act, stacked, preferred_element_type=jnp.float32).astype(
        jnp.bfloat16
    )
    heads_qkv = qkv.reshape(3, length, H, HS)
    query, keys, values = (heads_qkv[0], heads_qkv[1], heads_qkv[2])
    scale = 1.0 / math.sqrt(HS)
    scores = jnp.einsum("qhd,khd->hqk", query, keys, preferred_element_type=jnp.float32) * scale
    peak = jnp.max(scores, axis=-1, keepdims=True)
    expo = jnp.exp(scores - peak)
    probs = expo / jnp.sum(expo, axis=-1, keepdims=True)
    probs_b = probs.astype(jnp.bfloat16)
    attended = jnp.einsum("hqk,khd->qhd", probs_b, values, preferred_element_type=jnp.float32)
    attended = attended.reshape(length, width).astype(jnp.bfloat16)
    hidden = stream + jnp.dot(attended, w_out, preferred_element_type=jnp.float32)
    out_normed, rstd_out = norm_forward(hidden, dec_gains[1])
    out_b = out_normed.astype(jnp.bfloat16)
    pred = jnp.dot(out_b, head_weight, preferred_element_type=jnp.float32) + head_bias
    wanted = jnp.take(target_rows, positions, axis=0).astype(jnp.float32)
    error = (pred - wanted).astype(jnp.bfloat16)
    d_out = jnp.einsum("tp,cp->tc", error, head_weight, preferred_element_type=jnp.float32)
    d_hidden = norm_backward(hidden, rstd_out, dec_gains[1], d_out)
    d_hidden_b = d_hidden.astype(jnp.bfloat16)
    d_att = jnp.einsum("tc,ic->ti", d_hidden_b, w_out, preferred_element_type=jnp.float32).astype(
        jnp.bfloat16
    )
    d_att_h = d_att.reshape(length, H, HS)
    d_probs = jnp.einsum("qhd,khd->hqk", d_att_h, values, preferred_element_type=jnp.float32)
    d_values = jnp.einsum(
        "hqk,qhd->khd", probs_b, d_att_h, preferred_element_type=jnp.float32
    ).astype(jnp.bfloat16)
    d_scores = (
        probs * (d_probs - jnp.sum(d_probs * probs, axis=-1, keepdims=True)) * scale
    ).astype(jnp.bfloat16)
    d_query = jnp.einsum("hqk,khd->qhd", d_scores, keys, preferred_element_type=jnp.float32).astype(
        jnp.bfloat16
    )
    d_keys = jnp.einsum("hqk,qhd->khd", d_scores, query, preferred_element_type=jnp.float32).astype(
        jnp.bfloat16
    )
    d_qkv = jnp.stack([d_query, d_keys, d_values]).reshape(3, length, width)
    d_act = jnp.einsum("gto,gio->ti", d_qkv, stacked, preferred_element_type=jnp.float32)
    d_stream = d_hidden + norm_backward(stream, rstd_in, dec_gains[0], d_act)
    term_qkv = jnp.einsum("ti,gto->gio", act, d_qkv, preferred_element_type=jnp.float32).reshape(
        3 * width, width
    )
    term_out = jnp.einsum("ti,to->io", attended, d_hidden_b, preferred_element_type=jnp.float32)
    return (d_stream.astype(jnp.bfloat16), jnp.concatenate([term_qkv, term_out], 0))


def decoder_block(arrived, positions, target_rows, w_main, extras, total):
    samples, visible, width = arrived.shape

    def per_sample(carry, items):
        d_stream_b, term = decoder_sample(items[0], items[1], items[2], w_main, extras)
        return (carry + term, d_stream_b)

    total, d_streams = lax.scan(per_sample, total, (arrived, positions, target_rows))
    return (d_streams[:, :visible], d_streams.reshape(samples, visible, 4 * width), total)


def on_device(
    enc_input,
    weights,
    enc_gain,
    enc_bias,
    mask_token,
    pos_embed,
    dec_gains,
    head_weight,
    head_bias,
    order,
    targets,
):
    w_main = weights[0]
    micro, local, visible, wide = enc_input.shape
    width = w_main.shape[1]
    is_encoder = lax.axis_index("grp") == 0
    extras = (mask_token, pos_embed, dec_gains, head_weight, head_bias)
    total = jnp.zeros(w_main.shape, jnp.float32)
    blank_latent = jnp.zeros((local, visible, width), jnp.bfloat16)
    blank_normed = jnp.zeros((local, visible, wide), jnp.bfloat16)
    blank_rstd = jnp.zeros((local, visible, 1), jnp.float32)
    blanks = (blank_latent, blank_normed, blank_rstd)
    collected = []
    for step in range(micro):
        block = enc_input[step]
        latent, normed_b, rstd = lax.cond(
            is_encoder, lambda: encoder_forward(block, w_main, enc_gain, enc_bias), lambda: blanks
        )
        arrived = from_behind(latent, "grp", 1)
        d_latent, grads_dec, total = lax.cond(
            is_encoder,
            lambda: (blank_latent, blank_normed, total),
            lambda: decoder_block(arrived, order[step], targets[step], w_main, extras, total),
        )
        returned = from_behind(d_latent, "grp", -1)
        finished, total = lax.cond(
            is_encoder,
            lambda: encoder_backward(block, normed_b, rstd, w_main, enc_gain, returned, total),
            lambda: (grads_dec, total),
        )
        collected.append(finished)
    input_out = jnp.stack(collected)[None]
    dp_count = lax.axis_size("dp")
    section_count = lax.axis_size("section")
    count = micro * local * dp_count * section_count
    weight_out = reduce_scatter(total.astype(B16), 1.0 / count)[None]
    return (input_out, weight_out)


def solution(mesh):
    in_specs = (
        P(None, ("dp", "section"), None, None),
        P("grp", None, None),
        P(),
        P(),
        P(),
        P(),
        P(),
        P(),
        P(),
        P(None, ("dp", "section"), None),
        P(None, ("dp", "section"), None, None),
    )
    out_specs = (P("grp", None, ("dp", "section"), None, None), P("grp", ("dp", "section"), None))
    return jax.shard_map(
        on_device, mesh=mesh, in_specs=in_specs, out_specs=out_specs, check_vma=False
    )
```

```python
import functools
import math

import jax
import jax.numpy as jnp
from jax import lax
from jax.experimental import pallas as pl
from jax.experimental.pallas import tpu as pltpu
from jax.sharding import PartitionSpec as P

MESH = pl.DeviceIdType.MESH
B16 = jnp.bfloat16
F32 = jnp.float32
EPS = 1e-06
D = 1024
DE = 4096
L = 192
VIS = 48
HS = 64
ROWS = 2 * L
GROUP = 256
HEADS = GROUP // HS
NT = (((1,), (1,)), ((), ()))
TN = (((0,), (0,)), ((), ()))


def nn(a, b):
    return jnp.dot(a, b, preferred_element_type=F32)


def nt(a, b):
    return lax.dot_general(a, b, NT, preferred_element_type=F32)


def tn(a, b):
    return lax.dot_general(a, b, TN, preferred_element_type=F32)


def loop(n, body, unroll=1):
    def step(i, carry):
        body(i)
        return carry

    lax.fori_loop(0, n, step, 0, unroll=unroll)


def span(i, size):
    return pl.ds(pl.multiple_of(i * size, size), size)


def head_mask(h):
    return lax.broadcasted_iota(jnp.int32, (L, GROUP), 1) // HS == h


def stack_heads(block):
    zero = jnp.zeros_like(block)
    return jnp.concatenate([jnp.where(head_mask(h), block, zero) for h in range(HEADS)], 0)


def fold_heads(block):
    out = jnp.where(head_mask(0), block[:L], 0.0)
    for h in range(1, HEADS):
        out = jnp.where(head_mask(h), block[h * L : (h + 1) * L], out)
    return out


def norm_rows(values, gain):
    rstd = lax.rsqrt(jnp.mean(values * values, axis=-1, keepdims=True) + EPS)
    return values * rstd * gain


def norm_rows_back(values, gain, upstream):
    rstd = lax.rsqrt(jnp.mean(values * values, axis=-1, keepdims=True) + EPS)
    scaled = upstream * gain
    inner = jnp.mean(scaled * values, axis=-1, keepdims=True)
    return rstd * scaled - values * (rstd * rstd * rstd) * inner


class Ax:
    def __init__(self, view, r1, r2, ss, rs, plus, minus, send):
        self.view, self.r1, self.r2 = view, r1, r2
        self.ss, self.rs, self.plus, self.minus, self.send = ss, rs, plus, minus, send

    def half(self, ref, h):
        n = ref.shape[0] // 2
        return ref.at[pl.ds(h * n, n)]

    def go(self, src, dst, k, who):
        return self.send(src, dst, self.ss.at[k], self.rs.at[k], who)

    def step1(self):
        self.c0 = self.go(self.half(self.view(0), 0), self.r1.at[0], 0, self.plus)
        self.c1 = self.go(self.half(self.view(0), 1), self.r1.at[1], 1, self.minus)

    def step2(self):
        self.c2 = self.go(self.half(self.view(1), 1), self.half(self.r2.at[0], 1), 2, self.plus)
        self.c3 = self.go(self.half(self.view(2), 0), self.half(self.r2.at[1], 0), 3, self.minus)

    def step3(self):
        self.c0.wait_recv()
        mine = self.half(self.view(1), 0)
        mine[...] = mine[...] + self.r1[0]
        self.c4 = self.go(mine, self.half(self.r2.at[0], 0), 4, self.plus)
        self.c1.wait_recv()
        mine = self.half(self.view(2), 1)
        mine[...] = mine[...] + self.r1[1]
        self.c5 = self.go(mine, self.half(self.r2.at[1], 1), 5, self.minus)

    def finish_waits(self):
        for copy in (self.c2, self.c3, self.c4, self.c5):
            copy.wait_recv()


def kernel(
    scale,
    x_hbm, w_hbm, enc_gain, enc_bias, mask_token, pos_hbm, dec_gains, head_hbm, head_bias, order, tgt_hbm,
    g_out, w_out,
    w, pos, head, tgt, lat, lat_in, dlat, dlat_in,
    xb, normed, normed_t, rstd, acc, d_norm,
    stream, hidden, d_hidden, d_stream, tall, act, q, k, v, att, out_b, d_att, back, at, probs, wanted, err, gbuf,
    term, core_x, core_y, r1_x, r1_y, r2_x, r2_y, acc2_x, acc2_y, s1_x, s1_y, s2_x, s2_y, zr,
    w_sem, in_sem, out_sem, grp_send, grp_recv,
    core_send, core_recv, ssem, rsem, ssem2, rsem2, zsend, zrecv,
):
    dp = lax.axis_index("dp")
    x = lax.axis_index("section")
    grp = lax.axis_index("grp")
    y = dp // 4
    z = (dp // 2) % 2
    c = dp % 2

    def at_y(t):
        return {"dp": t * 4 + z * 2 + c}

    def at_x(t):
        return {"section": t}

    to_core = {"dp": y * 4 + z * 2 + (1 - c)}
    to_z = {"dp": y * 4 + (1 - z) * 2 + c}
    to_grp = {"grp": 1 - grp}
    xs = [(x + 2) % 4, (x + 1) % 4, (x + 3) % 4, x]
    ys = [(y + 2) % 4, (y + 1) % 4, (y + 3) % 4, y]

    barrier = pltpu.get_barrier_semaphore()
    for who in (to_grp, to_core, to_z, at_x(xs[1]), at_x(xs[2]), at_y(ys[1]), at_y(ys[2])):
        pl.semaphore_signal(barrier, inc=1, device_id=who, device_id_type=MESH)

    def remote(src, dst, send, recv, who):
        return pltpu.make_async_remote_copy(
            src_ref=src, dst_ref=dst, send_sem=send, recv_sem=recv, device_id=who, device_id_type=MESH
        )

    def w_copy(i):
        rows = pl.ds(pl.multiple_of(i * 512, 512), 512)
        return pltpu.make_async_copy(w_hbm.at[rows], w.at[rows], w_sem.at[i])

    x_copy = pltpu.make_async_copy(x_hbm, xb, in_sem.at[0])
    pos_copy = pltpu.make_async_copy(pos_hbm, pos, in_sem.at[1])
    head_copy = pltpu.make_async_copy(head_hbm, head, in_sem.at[2])
    tgt_copy = pltpu.make_async_copy(tgt_hbm, tgt, in_sem.at[3])
    lat_copy = remote(lat, lat_in, grp_send.at[0], grp_recv.at[0], to_grp)
    dlat_copy = remote(dlat, dlat_in, grp_send.at[1], grp_recv.at[1], to_grp)
    g_copy = pltpu.make_async_copy(gbuf, g_out, out_sem.at[0])

    @pl.when(grp == 0)
    def _():
        x_copy.start()

    @pl.when(grp == 1)
    def _():
        pos_copy.start()

    for i in range(8):
        w_copy(i).start()

    @pl.when(grp == 0)
    def _():
        x_copy.wait()
        squares = jnp.zeros((2 * VIS, 128), F32)
        for j in range(DE // 128):
            part = xb[:, j * 128 : (j + 1) * 128].astype(F32)
            squares = squares + part * part
        rs = lax.rsqrt(jnp.sum(squares, axis=-1, keepdims=True) * (1.0 / DE) + EPS)
        rstd[...] = jnp.broadcast_to(rs, (2 * VIS, 128))
        acc[...] = jnp.broadcast_to(enc_bias[...], (2 * VIS, D))

        def step(i):
            cols = span(i, 512)
            block = xb[:, cols].astype(F32) * rstd[:, 0:1] * enc_gain[:, cols]
            block = block.astype(B16)
            normed[:, cols] = block
            w_copy(i).wait()
            acc[...] += nn(block, w[cols, :])

        loop(8, step)
        lat[...] = acc[...].astype(B16)

    @pl.when(grp == 1)
    def _():
        tgt_copy.start()
        head_copy.start()
        pos_copy.wait()

        def onehot(s):
            rows = lax.broadcasted_iota(jnp.int32, (L, L), 0)
            return jnp.where(rows == order[s, 0:1, :], 1.0, 0.0).astype(B16)

        for s in range(2):
            hot = onehot(s)

            def gather(i):
                cols = span(i, 256)
                table = pos[:, cols]
                hi = table.astype(B16)
                rest = table - hi.astype(F32)
                mid = rest.astype(B16)
                low = (rest - mid.astype(F32)).astype(B16)
                rows = (tn(hot, hi) + tn(hot, mid)) + tn(hot, low)
                stream[s * L : s * L + VIS, cols] = rows[:VIS]
                stream[s * L + VIS : (s + 1) * L, cols] = rows[VIS:] + mask_token[:, cols]

            loop(4, gather)
        tgt_copy.wait()
        for s in range(2):
            wanted[s * L : (s + 1) * L, :] = tn(onehot(s), tgt[s]).astype(B16)
        gain = dec_gains[0:1, :]
        for s in range(2):

            def norms(i):
                rows = pl.ds(pl.multiple_of(s * L + VIS + i * 48, 16), 48)
                act[rows, :] = norm_rows(stream[rows, :], gain).astype(B16)

            loop(3, norms)
        for i in range(6):
            w_copy(i).wait()
        for part, dst in enumerate((q, k, v)):
            for s in range(2):

                def project(i):
                    cols = span(i, 256)
                    rows = pl.ds(s * L + VIS, L - VIS)
                    dst[rows, cols] = nn(act[rows, :], w[part * D : (part + 1) * D, cols]).astype(B16)

                loop(4, project)
        for i in range(6, 8):
            w_copy(i).wait()
        head_copy.wait()

    pl.semaphore_wait(barrier, 7)

    @pl.when(grp == 0)
    def _():
        lat_copy.start()

        def flip(i):
            cols = span(i, 512)
            normed_t[cols, :] = normed[:, cols].T

        loop(8, flip)
        lat_copy.wait_send()

    @pl.when(grp == 1)
    def _():
        lat_copy.wait_recv()
        gain = dec_gains[0:1, :]
        for s in range(2):
            rows = slice(s * L, s * L + VIS)
            value = stream[rows, :] + lat_in[s * VIS : (s + 1) * VIS, :].astype(F32)
            stream[rows, :] = value
            act[rows, :] = norm_rows(value, gain).astype(B16)
        for part, dst in enumerate((q, k, v)):

            def project(i):
                cols = span(i, 256)
                both = jnp.concatenate([act[:VIS, :], act[L : L + VIS, :]], 0)
                value = nn(both, w[part * D : (part + 1) * D, cols]).astype(B16)
                dst[:VIS, cols] = value[:VIS]
                dst[L : L + VIS, cols] = value[VIS:]

            loop(4, project)

        shrink = 1.0 / math.sqrt(HS)

        def attend(i):
            rows = span(i // 4, L)
            cols = span(i % 4, GROUP)
            scores = nt(stack_heads(q[rows, cols]), k[rows, cols]) * shrink
            expo = jnp.exp(scores - jnp.max(scores, axis=-1, keepdims=True))
            p = expo / jnp.sum(expo, axis=-1, keepdims=True)
            probs[i] = p
            att[rows, cols] = fold_heads(nn(p.astype(B16), v[rows, cols])).astype(B16)

        loop(8, attend)

        def out_proj(i):
            cols = span(i, 256)
            hidden[:, cols] = stream[:, cols] + nn(att[...], w[3 * D :, cols])

        loop(4, out_proj)
        gain_out = dec_gains[1:2, :]

        def out_norm(i):
            rows = span(i, 48)
            out_b[rows, :] = norm_rows(hidden[rows, :], gain_out).astype(B16)

        loop(8, out_norm)

        def pixel_head(i):
            rows = span(i, L)
            pred = nn(out_b[rows, :], head[...]) + head_bias[...]
            err[rows, :] = (pred - wanted[rows, :].astype(F32)).astype(B16)

        loop(2, pixel_head)

        def head_back(i):
            rows = span(i, 96)
            d_out = nt(err[rows, :], head[...])
            value = norm_rows_back(hidden[rows, :], gain_out, d_out)
            d_hidden[rows, :] = value
            back[3, rows, :] = value.astype(B16)

        loop(4, head_back)

        def att_back(i):
            cols = span(i, 256)
            d_att[:, cols] = nt(back[3], w[pl.ds(pl.multiple_of(3 * D + i * 256, 256), 256), :]).astype(B16)

        loop(4, att_back)

        def attend_back(i):
            rows = span(i // 4, L)
            cols = span(i % 4, GROUP)
            p = probs[i]
            up = stack_heads(d_att[rows, cols])
            d_p = nt(up, v[rows, cols])
            d_s = p * (d_p - jnp.sum(d_p * p, axis=-1, keepdims=True)) * shrink
            d_s = d_s.astype(B16)
            back[2, rows, cols] = tn(p.astype(B16), up).astype(B16)
            back[0, rows, cols] = fold_heads(nn(d_s, k[rows, cols])).astype(B16)
            back[1, rows, cols] = tn(d_s, stack_heads(q[rows, cols])).astype(B16)

        loop(8, attend_back)

        def act_back(i):
            cols = span(i, 256)
            total = nt(back[0], w[pl.ds(pl.multiple_of(i * 256, 256), 256), :])
            total = total + nt(back[1], w[pl.ds(pl.multiple_of(D + i * 256, 256), 256), :])
            total = total + nt(back[2], w[pl.ds(pl.multiple_of(2 * D + i * 256, 256), 256), :])
            d_stream[:, cols] = total

        loop(4, act_back)

        def stream_back(i):
            rows = span(i, 48)
            value = d_hidden[rows, :] + norm_rows_back(stream[rows, :], gain, d_stream[rows, :])
            for t in range(8):
                tall[t, rows, :] = value[:, t * 128 : (t + 1) * 128]

            @pl.when(i % 4 == 0)
            def _():
                dlat[span(i // 4, VIS), :] = value.astype(B16)

        loop(8, stream_back)
        dlat_copy.start()
        at[0] = act[...].T
        at[1] = att[...].T

        def terms(i):
            blk = i // 4
            value = nn(at[blk // 3, span(i % 4, 256), :], back[blk])
            term[i // 4, (i // 2) % 2, i % 2] = value.astype(B16).reshape(4, 64, D)

        loop(16, terms)
        for s in range(2):
            for j in range(4):
                for t in range(8):
                    start = j * D + t * 128
                    gbuf[s, :, start : start + 128] = tall[t, pl.ds(s * L + j, VIS, stride=4), :].astype(B16)
        g_copy.start()
        dlat_copy.wait_send()

    @pl.when(grp == 0)
    def _():
        dlat_copy.wait_recv()

        def terms(i):
            value = nn(normed_t[span(i, 256), :], dlat_in[...])
            term[i // 4, (i // 2) % 2, i % 2] = value.astype(B16).reshape(4, 64, D)

        loop(16, terms)

    def send(src, dst, send_s, recv_s, who):
        copy = remote(src, dst, send_s, recv_s, who)
        copy.start()
        started.append(copy)
        return copy

    started = []

    def px(j, core):
        return term.at[:, :, core, xs[j], pl.ds(0, 32)]

    def py(j, core):
        return term.at[ys[j], :, core, :, pl.ds(32, 32)]

    parts = (px, py)
    corebufs = (core_x, core_y)
    cores = {}
    for a, j in ((0, 0), (1, 0), (0, 1), (0, 2), (1, 1), (1, 2), (0, 3), (1, 3)):
        cores[a, j] = send(
            parts[a](j, 1 - c), corebufs[a].at[j], core_send.at[a, j], core_recv.at[a, j], to_core
        )

    def merge(a, j):
        cores[a, j].wait_recv()
        mine = parts[a](j, c)
        mine[...] = mine[...] + corebufs[a][j]

    first = (
        Ax(lambda j: px(j, c), r1_x, r2_x, ssem.at[0], rsem.at[0], at_x(xs[1]), at_x(xs[2]), send),
        Ax(lambda j: py(j, c), r1_y, r2_y, ssem.at[1], rsem.at[1], at_y(ys[1]), at_y(ys[2]), send),
    )
    second = (
        Ax(lambda j: acc2_x.at[j], s1_x, s2_x, ssem2.at[0], rsem2.at[0], at_y(ys[1]), at_y(ys[2]), send),
        Ax(lambda j: acc2_y.at[j], s1_y, s2_y, ssem2.at[1], rsem2.at[1], at_x(xs[1]), at_x(xs[2]), send),
    )
    for a in (0, 1):
        merge(a, 0)
        first[a].step1()
    for a in (0, 1):
        merge(a, 1)
        merge(a, 2)
        first[a].step2()
    @pl.when(grp == 0)
    def _():
        acc2 = jnp.zeros((2 * VIS, 1), F32)

        def step(i, inner):
            cols = span(i, 256)
            d_n = nt(dlat_in[...], w[cols, :])
            scaled = d_n * enc_gain[:, cols]
            d_norm[:, cols] = scaled
            return inner + jnp.sum(scaled * xb[:, cols].astype(F32), axis=-1, keepdims=True)

        inner = lax.fori_loop(0, 16, step, acc2) * (1.0 / DE)
        rs = rstd[:, 0:1]
        factor = rs * rs * rs * inner
        for i in range(8):
            cols = slice(i * 512, (i + 1) * 512)
            value = (rs * d_norm[:, cols] - xb[:, cols].astype(F32) * factor).astype(B16)
            gbuf[0, :, cols] = value[:VIS]
            gbuf[1, :, cols] = value[VIS:]
        g_copy.start()

    for a in (0, 1):
        first[a].step3()
    for a in (0, 1):
        merge(a, 3)

    def total(a, j):
        ax = first[a]
        if a == 0:
            rows = lambda ref: ref[ys[j]]
        else:
            rows = lambda ref: ref[:, xs[j]]
        value = rows(ax.view(3)).astype(F32) + rows(ax.r2.at[0]).astype(F32) + rows(ax.r2.at[1]).astype(F32)
        second[a].view(j)[...] = value.astype(B16)

    for a in (0, 1):
        first[a].finish_waits()
        total(a, 0)
        second[a].step1()
        total(a, 1)
        total(a, 2)
        second[a].step2()
        total(a, 3)
    for a in (0, 1):
        second[a].step3()
    zcopies = []
    for a in (0, 1):
        ax = second[a]
        ax.finish_waits()
        mine = ax.view(3)
        value = mine[...].astype(F32) + ax.r2[0].astype(F32) + ax.r2[1].astype(F32)
        mine[...] = value.astype(B16)
        zcopies.append(send(mine.at[1 - z], zr.at[a], zsend.at[a], zrecv.at[a], to_z))
    for a in (0, 1):
        zcopies[a].wait_recv()
        w_out[a * 32 : (a + 1) * 32, :] = (second[a].view(3)[z].astype(F32) + zr[a].astype(F32)) * scale
    g_copy.wait()
    for copy in started:
        copy.wait_send()


def on_device(
    enc_input, weights, enc_gain, enc_bias, mask_token, pos_embed, dec_gains, head_weight, head_bias, order, targets
):
    V = pltpu.VMEM
    S = pltpu.SemaphoreType.DMA
    full = pl.BlockSpec(memory_space=pltpu.VMEM)
    hbm = pl.BlockSpec(memory_space=pl.ANY)
    count = 2 * lax.axis_size("dp") * lax.axis_size("section")
    grads, w_grad = pl.pallas_call(
        functools.partial(kernel, 1.0 / count),
        out_shape=(jax.ShapeDtypeStruct((2, VIS, DE), B16), jax.ShapeDtypeStruct((64, D), F32)),
        in_specs=[hbm, hbm, full, full, full, hbm, full, hbm, full, full, hbm],
        out_specs=(hbm, full),
        scratch_shapes=[
            V((DE, D), B16), V((L, D), F32), V((D, 256), B16), V((2, L, 256), B16),
            V((2 * VIS, D), B16), V((2 * VIS, D), B16), V((2 * VIS, D), B16), V((2 * VIS, D), B16),
            V((2 * VIS, DE), B16), V((2 * VIS, DE), B16), V((DE, 2 * VIS), B16), V((2 * VIS, 128), F32),
            V((2 * VIS, D), F32), V((2 * VIS, DE), F32),
            V((ROWS, D), F32), V((ROWS, D), F32), V((ROWS, D), F32), V((ROWS, D), F32), V((8, ROWS, 128), F32),
            V((ROWS, D), B16), V((ROWS, D), B16), V((ROWS, D), B16), V((ROWS, D), B16), V((ROWS, D), B16),
            V((ROWS, D), B16), V((ROWS, D), B16), V((4, ROWS, D), B16), V((2, D, ROWS), B16),
            V((8, HEADS * L, L), F32), V((ROWS, 256), B16), V((ROWS, 256), B16), V((2, VIS, DE), B16),
            V((4, 2, 2, 4, 64, D), B16),
            V((4, 4, 2, 32, D), B16), V((4, 2, 4, 32, D), B16),
            V((2, 2, 2, 32, D), B16), V((2, 1, 4, 32, D), B16),
            V((2, 4, 2, 32, D), B16), V((2, 2, 4, 32, D), B16),
            V((4, 2, 32, D), B16), V((4, 2, 32, D), B16),
            V((2, 1, 32, D), B16), V((2, 1, 32, D), B16),
            V((2, 2, 32, D), B16), V((2, 2, 32, D), B16),
            V((2, 32, D), B16),
            S((8,)), S((4,)), S((1,)), S((2,)), S((2,)),
            S((2, 4)), S((2, 4)), S((2, 6)), S((2, 6)), S((2, 6)), S((2, 6)), S((2,)), S((2,)),
        ],
        compiler_params=pltpu.CompilerParams(
            collective_id=0, has_side_effects=True, vmem_limit_bytes=60 * 2**20
        ),
        name="window",
    )(
        enc_input.reshape(2 * VIS, DE), weights[0], enc_gain[None], enc_bias[None], mask_token[None], pos_embed,
        dec_gains, head_weight, head_bias[None], order, targets.reshape(2, L, 256),
    )
    return grads[None, :, None], w_grad[None]


def solution(mesh):
    many = ("dp", "section")
    in_specs = (
        P(None, many, None, None), P("grp", None, None), P(), P(), P(), P(), P(), P(), P(),
        P(None, many, None), P(None, many, None, None),
    )
    out_specs = (P("grp", None, many, None, None), P("grp", many, None))
    return jax.shard_map(on_device, mesh=mesh, in_specs=in_specs, out_specs=out_specs, check_vma=False)
```

```python
import functools
import math

import jax
import jax.numpy as jnp
from jax import lax
from jax.experimental import pallas as pl
from jax.experimental.pallas import tpu as pltpu
from jax.sharding import PartitionSpec as P

MESH = pl.DeviceIdType.MESH
B16 = jnp.bfloat16
F32 = jnp.float32
EPS = 1e-06
D = 1024
DE = 4096
L = 192
VIS = 48
HS = 64
ROWS = 2 * L
GROUP = 256
HEADS = GROUP // HS
NT = (((1,), (1,)), ((), ()))
TN = (((0,), (0,)), ((), ()))


def nn(a, b):
    return jnp.dot(a, b, preferred_element_type=F32)


def nt(a, b):
    return lax.dot_general(a, b, NT, preferred_element_type=F32)


def tn(a, b):
    return lax.dot_general(a, b, TN, preferred_element_type=F32)


def loop(n, body, unroll=1):
    def step(i, carry):
        body(i)
        return carry

    lax.fori_loop(0, n, step, 0, unroll=unroll)


def span(i, size):
    return pl.ds(pl.multiple_of(i * size, size), size)


def head_mask(h):
    return lax.broadcasted_iota(jnp.int32, (L, GROUP), 1) // HS == h


def stack_heads(block):
    zero = jnp.zeros_like(block)
    return jnp.concatenate([jnp.where(head_mask(h), block, zero) for h in range(HEADS)], 0)


def fold_heads(block):
    out = jnp.where(head_mask(0), block[:L], 0.0)
    for h in range(1, HEADS):
        out = jnp.where(head_mask(h), block[h * L : (h + 1) * L], out)
    return out


def norm_rows(values, gain):
    rstd = lax.rsqrt(jnp.mean(values * values, axis=-1, keepdims=True) + EPS)
    return values * rstd * gain


def norm_rows_back(values, gain, upstream):
    rstd = lax.rsqrt(jnp.mean(values * values, axis=-1, keepdims=True) + EPS)
    scaled = upstream * gain
    inner = jnp.mean(scaled * values, axis=-1, keepdims=True)
    return rstd * scaled - values * (rstd * rstd * rstd) * inner


class Ax:
    def __init__(self, view, r1, r2, ss, rs, plus, minus, send):
        self.view, self.r1, self.r2 = view, r1, r2
        self.ss, self.rs, self.plus, self.minus, self.send = ss, rs, plus, minus, send

    def half(self, ref, h):
        n = ref.shape[0] // 2
        return ref.at[pl.ds(h * n, n)]

    def go(self, src, dst, k, who):
        return self.send(src, dst, self.ss.at[k], self.rs.at[k], who)

    def step1(self):
        self.c0 = self.go(self.half(self.view(0), 0), self.r1.at[0], 0, self.plus)
        self.c1 = self.go(self.half(self.view(0), 1), self.r1.at[1], 1, self.minus)

    def step2(self):
        self.c2 = self.go(self.half(self.view(1), 1), self.half(self.r2.at[0], 1), 2, self.plus)
        self.c3 = self.go(self.half(self.view(2), 0), self.half(self.r2.at[1], 0), 3, self.minus)

    def step3(self):
        self.c0.wait_recv()
        mine = self.half(self.view(1), 0)
        mine[...] = mine[...] + self.r1[0]
        self.c4 = self.go(mine, self.half(self.r2.at[0], 0), 4, self.plus)
        self.c1.wait_recv()
        mine = self.half(self.view(2), 1)
        mine[...] = mine[...] + self.r1[1]
        self.c5 = self.go(mine, self.half(self.r2.at[1], 1), 5, self.minus)

    def finish_waits(self):
        for copy in (self.c2, self.c3, self.c4, self.c5):
            copy.wait_recv()


def kernel(
    scale,
    x_hbm, w_hbm, enc_gain, enc_bias, mask_token, pos_hbm, dec_gains, head_hbm, head_bias, order, tgt_hbm,
    g_out, w_out,
    w, pos, head, tgt, lat, lat_in, dlat, dlat_in,
    xb, normed, normed_t, rstd, acc, d_norm,
    stream, hidden, d_hidden, d_stream, tall, act, act_m, act_v, q, k, v, att, out_b, d_att, back, at, probs, wanted, err, gbuf,
    term, core_x, core_y, r1_x, r1_y, r2_x, r2_y, acc2_x, acc2_y, s1_x, s1_y, s2_x, s2_y, zr,
    w_sem, in_sem, out_sem, grp_send, grp_recv,
    core_send, core_recv, ssem, rsem, ssem2, rsem2, zsend, zrecv,
):
    dp = lax.axis_index("dp")
    x = lax.axis_index("section")
    grp = lax.axis_index("grp")
    y = dp // 4
    z = (dp // 2) % 2
    c = dp % 2

    def at_y(t):
        return {"dp": t * 4 + z * 2 + c}

    def at_x(t):
        return {"section": t}

    to_core = {"dp": y * 4 + z * 2 + (1 - c)}
    to_z = {"dp": y * 4 + (1 - z) * 2 + c}
    to_grp = {"grp": 1 - grp}
    xs = [(x + 2) % 4, (x + 1) % 4, (x + 3) % 4, x]
    ys = [(y + 2) % 4, (y + 1) % 4, (y + 3) % 4, y]

    barrier = pltpu.get_barrier_semaphore()
    for who in (to_grp, to_core, to_z, at_x(xs[1]), at_x(xs[2]), at_y(ys[1]), at_y(ys[2])):
        pl.semaphore_signal(barrier, inc=1, device_id=who, device_id_type=MESH)

    def remote(src, dst, send, recv, who):
        return pltpu.make_async_remote_copy(
            src_ref=src, dst_ref=dst, send_sem=send, recv_sem=recv, device_id=who, device_id_type=MESH
        )

    def w_copy(i):
        rows = pl.ds(pl.multiple_of(i * 512, 512), 512)
        return pltpu.make_async_copy(w_hbm.at[rows], w.at[rows], w_sem.at[i])

    x_copy = pltpu.make_async_copy(x_hbm, xb, in_sem.at[0])
    pos_copy = pltpu.make_async_copy(pos_hbm, pos, in_sem.at[1])
    head_copy = pltpu.make_async_copy(head_hbm, head, in_sem.at[2])
    tgt_copy = pltpu.make_async_copy(tgt_hbm, tgt, in_sem.at[3])
    lat_copy = remote(lat, lat_in, grp_send.at[0], grp_recv.at[0], to_grp)
    dlat_copy = remote(dlat, dlat_in, grp_send.at[1], grp_recv.at[1], to_grp)
    g_copy = pltpu.make_async_copy(gbuf, g_out, out_sem.at[0])

    @pl.when(grp == 0)
    def _():
        x_copy.start()

    @pl.when(grp == 1)
    def _():
        pos_copy.start()

    for i in range(8):
        w_copy(i).start()

    @pl.when(grp == 0)
    def _():
        x_copy.wait()
        squares = jnp.zeros((2 * VIS, 128), F32)
        for j in range(DE // 128):
            part = xb[:, j * 128 : (j + 1) * 128].astype(F32)
            squares = squares + part * part
        rs = lax.rsqrt(jnp.sum(squares, axis=-1, keepdims=True) * (1.0 / DE) + EPS)
        rstd[...] = jnp.broadcast_to(rs, (2 * VIS, 128))
        acc[...] = jnp.broadcast_to(enc_bias[...], (2 * VIS, D))

        def step(i):
            cols = span(i, 512)
            block = xb[:, cols].astype(F32) * rstd[:, 0:1] * enc_gain[:, cols]
            block = block.astype(B16)
            normed[:, cols] = block
            w_copy(i).wait()
            acc[...] += nn(block, w[cols, :])

        loop(8, step, 8)
        lat[...] = acc[...].astype(B16)

    @pl.when(grp == 1)
    def _():
        tgt_copy.start()
        head_copy.start()
        pos_copy.wait()

        hi = pos[...].astype(B16)
        rest = pos[...] - hi.astype(F32)
        mid = rest.astype(B16)
        low = (rest - mid.astype(F32)).astype(B16)
        gain = dec_gains[0:1, :]
        hots = []
        for s in range(2):
            rows = lax.broadcasted_iota(jnp.int32, (L, L), 0)
            hot = jnp.where(rows == order[s, 0:1, :], 1.0, 0.0).T.astype(B16)
            hots.append(hot)
            found = (nn(hot, hi) + nn(hot, mid)) + nn(hot, low)
            stream[s * L : s * L + VIS, :] = found[:VIS]
            value = found[VIS:] + mask_token[...]
            stream[s * L + VIS : (s + 1) * L, :] = value
            normal = norm_rows(value, gain).astype(B16)
            act[s * L + VIS : (s + 1) * L, :] = normal
            act_m[s * (L - VIS) : (s + 1) * (L - VIS), :] = normal
        for part, dst in enumerate((q, k, v)):
            w_copy(2 * part).wait()
            w_copy(2 * part + 1).wait()
            value = nn(act_m[...], w[part * D : (part + 1) * D, :]).astype(B16)
            dst[VIS:L, :] = value[: L - VIS]
            dst[L + VIS :, :] = value[L - VIS :]
        tgt_copy.wait()
        for s in range(2):
            wanted[s * L : (s + 1) * L, :] = nn(hots[s], tgt[s]).astype(B16)
        for i in range(6, 8):
            w_copy(i).wait()
        head_copy.wait()

    pl.semaphore_wait(barrier, 7)

    @pl.when(grp == 0)
    def _():
        lat_copy.start()

        def flip(i):
            cols = span(i, 512)
            normed_t[cols, :] = normed[:, cols].T

        loop(8, flip, 4)
        lat_copy.wait_send()

    @pl.when(grp == 1)
    def _():
        lat_copy.wait_recv()
        gain = dec_gains[0:1, :]
        for s in range(2):
            rows = slice(s * L, s * L + VIS)
            value = stream[rows, :] + lat_in[s * VIS : (s + 1) * VIS, :].astype(F32)
            stream[rows, :] = value
            normal = norm_rows(value, gain).astype(B16)
            act[rows, :] = normal
            act_v[s * VIS : (s + 1) * VIS, :] = normal
        for part, dst in enumerate((q, k, v)):
            value = nn(act_v[...], w[part * D : (part + 1) * D, :]).astype(B16)
            dst[:VIS, :] = value[:VIS]
            dst[L : L + VIS, :] = value[VIS:]

        shrink = 1.0 / math.sqrt(HS)

        def attend(i):
            rows = span(i // 4, L)
            cols = span(i % 4, GROUP)
            scores = nt(stack_heads(q[rows, cols]), k[rows, cols]) * shrink
            expo = jnp.exp(scores - jnp.max(scores, axis=-1, keepdims=True))
            p = expo * (1.0 / jnp.sum(expo, axis=-1, keepdims=True))
            probs[i] = p
            att[rows, cols] = fold_heads(nn(p.astype(B16), v[rows, cols])).astype(B16)

        loop(8, attend, 8)

        hidden[...] = stream[...] + nn(att[...], w[3 * D :, :])
        gain_out = dec_gains[1:2, :]

        def head_both(i):
            rows = span(i, L)
            out_b[rows, :] = norm_rows(hidden[rows, :], gain_out).astype(B16)
            pred = nn(out_b[rows, :], head[...]) + head_bias[...]
            err[rows, :] = (pred - wanted[rows, :].astype(F32)).astype(B16)
            value = norm_rows_back(hidden[rows, :], gain_out, nt(err[rows, :], head[...]))
            d_hidden[rows, :] = value
            back[3, rows, :] = value.astype(B16)

        loop(2, head_both, 2)
        d_att[...] = nt(back[3], w[3 * D :, :]).astype(B16)

        def attend_back(i):
            rows = span(i // 4, L)
            cols = span(i % 4, GROUP)
            p = probs[i]
            up = stack_heads(d_att[rows, cols])
            d_p = nt(up, v[rows, cols])
            d_s = p * (d_p - jnp.sum(d_p * p, axis=-1, keepdims=True)) * shrink
            d_s = d_s.astype(B16)
            back[2, rows, cols] = tn(p.astype(B16), up).astype(B16)
            back[0, rows, cols] = fold_heads(nn(d_s, k[rows, cols])).astype(B16)
            back[1, rows, cols] = tn(d_s, stack_heads(q[rows, cols])).astype(B16)

        loop(8, attend_back, 8)

        for i in range(2):
            cols = slice(i * 512, (i + 1) * 512)
            total = nt(back[0], w[i * 512 : (i + 1) * 512, :])
            total = total + nt(back[1], w[D + i * 512 : D + (i + 1) * 512, :])
            d_stream[:, cols] = total + nt(back[2], w[2 * D + i * 512 : 2 * D + (i + 1) * 512, :])

        def stream_back(i):
            rows = span(i, 48)
            value = d_hidden[rows, :] + norm_rows_back(stream[rows, :], gain, d_stream[rows, :])
            for t in range(8):
                tall[t, rows, :] = value[:, t * 128 : (t + 1) * 128]

            @pl.when(i % 4 == 0)
            def _():
                dlat[span(i // 4, VIS), :] = value.astype(B16)

        loop(8, stream_back, 4)
        dlat_copy.start()
        at[0] = act[...].T
        at[1] = att[...].T

        def terms(i):
            blk = i // 4
            value = nn(at[blk // 3, span(i % 4, 256), :], back[blk])
            term[i // 4, (i // 2) % 2, i % 2] = value.astype(B16).reshape(4, 64, D)

        loop(16, terms, 4)
        for s in range(2):
            for j in range(4):
                for t in range(8):
                    start = j * D + t * 128
                    gbuf[s, :, start : start + 128] = tall[t, pl.ds(s * L + j, VIS, stride=4), :].astype(B16)
        g_copy.start()
        dlat_copy.wait_send()

    @pl.when(grp == 0)
    def _():
        dlat_copy.wait_recv()

        def terms(i):
            value = nn(normed_t[span(i, 256), :], dlat_in[...])
            term[i // 4, (i // 2) % 2, i % 2] = value.astype(B16).reshape(4, 64, D)

        loop(16, terms, 8)

    def send(src, dst, send_s, recv_s, who):
        copy = remote(src, dst, send_s, recv_s, who)
        copy.start()
        started.append(copy)
        return copy

    started = []

    def px(j, core):
        return term.at[:, :, core, xs[j], pl.ds(0, 32)]

    def py(j, core):
        return term.at[ys[j], :, core, :, pl.ds(32, 32)]

    parts = (px, py)
    corebufs = (core_x, core_y)
    cores = {}
    for a, j in ((0, 0), (1, 0), (0, 1), (0, 2), (1, 1), (1, 2), (0, 3), (1, 3)):
        cores[a, j] = send(
            parts[a](j, 1 - c), corebufs[a].at[j], core_send.at[a, j], core_recv.at[a, j], to_core
        )

    def merge(a, j):
        cores[a, j].wait_recv()
        mine = parts[a](j, c)
        mine[...] = mine[...] + corebufs[a][j]

    first = (
        Ax(lambda j: px(j, c), r1_x, r2_x, ssem.at[0], rsem.at[0], at_x(xs[1]), at_x(xs[2]), send),
        Ax(lambda j: py(j, c), r1_y, r2_y, ssem.at[1], rsem.at[1], at_y(ys[1]), at_y(ys[2]), send),
    )
    second = (
        Ax(lambda j: acc2_x.at[j], s1_x, s2_x, ssem2.at[0], rsem2.at[0], at_y(ys[1]), at_y(ys[2]), send),
        Ax(lambda j: acc2_y.at[j], s1_y, s2_y, ssem2.at[1], rsem2.at[1], at_x(xs[1]), at_x(xs[2]), send),
    )
    for a in (0, 1):
        merge(a, 0)
        first[a].step1()
    for a in (0, 1):
        merge(a, 1)
        merge(a, 2)
        first[a].step2()
    @pl.when(grp == 0)
    def _():
        acc2 = jnp.zeros((2 * VIS, 1), F32)

        def step(i, inner):
            cols = span(i, 256)
            d_n = nt(dlat_in[...], w[cols, :])
            scaled = d_n * enc_gain[:, cols]
            d_norm[:, cols] = scaled
            return inner + jnp.sum(scaled * xb[:, cols].astype(F32), axis=-1, keepdims=True)

        inner = lax.fori_loop(0, 16, step, acc2, unroll=4) * (1.0 / DE)
        rs = rstd[:, 0:1]
        factor = rs * rs * rs * inner
        for i in range(8):
            cols = slice(i * 512, (i + 1) * 512)
            value = (rs * d_norm[:, cols] - xb[:, cols].astype(F32) * factor).astype(B16)
            gbuf[0, :, cols] = value[:VIS]
            gbuf[1, :, cols] = value[VIS:]
        g_copy.start()

    for a in (0, 1):
        first[a].step3()
    for a in (0, 1):
        merge(a, 3)

    def total(a, j):
        ax = first[a]
        if a == 0:
            rows = lambda ref: ref[ys[j]]
        else:
            rows = lambda ref: ref[:, xs[j]]
        value = rows(ax.view(3)).astype(F32) + rows(ax.r2.at[0]).astype(F32) + rows(ax.r2.at[1]).astype(F32)
        second[a].view(j)[...] = value.astype(B16)

    for a in (0, 1):
        first[a].finish_waits()
        total(a, 0)
        second[a].step1()
        total(a, 1)
        total(a, 2)
        second[a].step2()
        total(a, 3)
    for a in (0, 1):
        second[a].step3()
    zcopies = []
    for a in (0, 1):
        ax = second[a]
        ax.finish_waits()
        mine = ax.view(3)
        value = mine[...].astype(F32) + ax.r2[0].astype(F32) + ax.r2[1].astype(F32)
        mine[...] = value.astype(B16)
        zcopies.append(send(mine.at[1 - z], zr.at[a], zsend.at[a], zrecv.at[a], to_z))
    for a in (0, 1):
        zcopies[a].wait_recv()
        w_out[a * 32 : (a + 1) * 32, :] = (second[a].view(3)[z].astype(F32) + zr[a].astype(F32)) * scale
    g_copy.wait()
    for copy in started:
        copy.wait_send()


def on_device(
    enc_input, weights, enc_gain, enc_bias, mask_token, pos_embed, dec_gains, head_weight, head_bias, order, targets
):
    V = pltpu.VMEM
    S = pltpu.SemaphoreType.DMA
    full = pl.BlockSpec(memory_space=pltpu.VMEM)
    hbm = pl.BlockSpec(memory_space=pl.ANY)
    count = 2 * lax.axis_size("dp") * lax.axis_size("section")
    grads, w_grad = pl.pallas_call(
        functools.partial(kernel, 1.0 / count),
        out_shape=(jax.ShapeDtypeStruct((2, VIS, DE), B16), jax.ShapeDtypeStruct((64, D), F32)),
        in_specs=[hbm, hbm, full, full, full, hbm, full, hbm, full, full, hbm],
        out_specs=(hbm, full),
        scratch_shapes=[
            V((DE, D), B16), V((L, D), F32), V((D, 256), B16), V((2, L, 256), B16),
            V((2 * VIS, D), B16), V((2 * VIS, D), B16), V((2 * VIS, D), B16), V((2 * VIS, D), B16),
            V((2 * VIS, DE), B16), V((2 * VIS, DE), B16), V((DE, 2 * VIS), B16), V((2 * VIS, 128), F32),
            V((2 * VIS, D), F32), V((2 * VIS, DE), F32),
            V((ROWS, D), F32), V((ROWS, D), F32), V((ROWS, D), F32), V((ROWS, D), F32), V((8, ROWS, 128), F32),
            V((ROWS, D), B16), V((ROWS - 2 * VIS, D), B16), V((2 * VIS, D), B16),
            V((ROWS, D), B16), V((ROWS, D), B16), V((ROWS, D), B16), V((ROWS, D), B16),
            V((ROWS, D), B16), V((ROWS, D), B16), V((4, ROWS, D), B16), V((2, D, ROWS), B16),
            V((8, HEADS * L, L), F32), V((ROWS, 256), B16), V((ROWS, 256), B16), V((2, VIS, DE), B16),
            V((4, 2, 2, 4, 64, D), B16),
            V((4, 4, 2, 32, D), B16), V((4, 2, 4, 32, D), B16),
            V((2, 2, 2, 32, D), B16), V((2, 1, 4, 32, D), B16),
            V((2, 4, 2, 32, D), B16), V((2, 2, 4, 32, D), B16),
            V((4, 2, 32, D), B16), V((4, 2, 32, D), B16),
            V((2, 1, 32, D), B16), V((2, 1, 32, D), B16),
            V((2, 2, 32, D), B16), V((2, 2, 32, D), B16),
            V((2, 32, D), B16),
            S((8,)), S((4,)), S((1,)), S((2,)), S((2,)),
            S((2, 4)), S((2, 4)), S((2, 6)), S((2, 6)), S((2, 6)), S((2, 6)), S((2,)), S((2,)),
        ],
        compiler_params=pltpu.CompilerParams(
            collective_id=0, has_side_effects=True, vmem_limit_bytes=60 * 2**20
        ),
        name="window",
    )(
        enc_input.reshape(2 * VIS, DE), weights[0], enc_gain[None], enc_bias[None], mask_token[None], pos_embed,
        dec_gains, head_weight, head_bias[None], order, targets.reshape(2, L, 256),
    )
    return grads[None, :, None], w_grad[None]


def solution(mesh):
    many = ("dp", "section")
    in_specs = (
        P(None, many, None, None), P("grp", None, None), P(), P(), P(), P(), P(), P(), P(),
        P(None, many, None), P(None, many, None, None),
    )
    out_specs = (P("grp", None, many, None, None), P("grp", many, None))
    return jax.shard_map(on_device, mesh=mesh, in_specs=in_specs, out_specs=out_specs, check_vma=False)
```

```python
import functools
import math

import jax
import jax.numpy as jnp
from jax import lax
from jax.experimental import pallas as pl
from jax.experimental.pallas import tpu as pltpu
from jax.sharding import PartitionSpec as P

MESH = pl.DeviceIdType.MESH
B16 = jnp.bfloat16
F32 = jnp.float32
EPS = 1e-06
D = 1024
DE = 4096
L = 192
VIS = 48
HS = 64
ROWS = 2 * L
GROUP = 256
HEADS = GROUP // HS
NT = (((1,), (1,)), ((), ()))
TN = (((0,), (0,)), ((), ()))


def nn(a, b):
    return jnp.dot(a, b, preferred_element_type=F32)


def nt(a, b):
    return lax.dot_general(a, b, NT, preferred_element_type=F32)


def tn(a, b):
    return lax.dot_general(a, b, TN, preferred_element_type=F32)


def loop(n, body, unroll=1):
    def step(i, carry):
        body(i)
        return carry

    lax.fori_loop(0, n, step, 0, unroll=unroll)


def span(i, size):
    return pl.ds(pl.multiple_of(i * size, size), size)


def head_mask(h):
    return lax.broadcasted_iota(jnp.int32, (L, GROUP), 1) // HS == h


def stack_heads(block):
    zero = jnp.zeros_like(block)
    return jnp.concatenate([jnp.where(head_mask(h), block, zero) for h in range(HEADS)], 0)


def fold_heads(block):
    out = jnp.where(head_mask(0), block[:L], 0.0)
    for h in range(1, HEADS):
        out = jnp.where(head_mask(h), block[h * L : (h + 1) * L], out)
    return out


def norm_rows(values, gain):
    rstd = lax.rsqrt(jnp.mean(values * values, axis=-1, keepdims=True) + EPS)
    return values * rstd * gain


def norm_rows_back(values, gain, upstream):
    rstd = lax.rsqrt(jnp.mean(values * values, axis=-1, keepdims=True) + EPS)
    scaled = upstream * gain
    inner = jnp.mean(scaled * values, axis=-1, keepdims=True)
    return rstd * scaled - values * (rstd * rstd * rstd) * inner


class Chunk:
    def __init__(self, view, pick, r1, r2, acc, r3, sems, first, second, send):
        self.view, self.pick, self.r1, self.r2, self.acc, self.r3 = view, pick, r1, r2, acc, r3
        self.s1, self.v1, self.s2, self.v2 = sems
        self.first, self.second, self.send = first, second, send

    def half(self, ref, h):
        n = ref.shape[0] // 2
        return ref.at[pl.ds(h * n, n)]

    def go(self, src, dst, k, who):
        return self.send(src, dst, self.s1.at[k], self.v1.at[k], who)

    def step1(self):
        plus, minus = self.first[1:3]
        self.c0 = self.go(self.half(self.view(0), 0), self.r1.at[0], 0, plus)
        self.c1 = self.go(self.half(self.view(0), 1), self.r1.at[1], 1, minus)

    def step2(self):
        plus, minus = self.first[1:3]
        self.c2 = self.go(self.half(self.view(1), 1), self.half(self.r2.at[0], 1), 2, plus)
        self.c3 = self.go(self.half(self.view(2), 0), self.half(self.r2.at[1], 0), 3, minus)

    def step3(self):
        plus, minus = self.first[1:3]
        self.c0.wait_recv()
        mine = self.half(self.view(1), 0)
        mine[...] = mine[...] + self.r1[0]
        self.c4 = self.go(mine, self.half(self.r2.at[0], 0), 4, plus)
        self.c1.wait_recv()
        mine = self.half(self.view(2), 1)
        mine[...] = mine[...] + self.r1[1]
        self.c5 = self.go(mine, self.half(self.r2.at[1], 1), 5, minus)

    def step4(self):
        for copy in (self.c2, self.c3, self.c4, self.c5):
            copy.wait_recv()
        self.direct = []
        for j in range(4):
            value = self.pick(self.view(3), j).astype(F32)
            value = value + self.pick(self.r2.at[0], j).astype(F32) + self.pick(self.r2.at[1], j).astype(F32)
            self.acc[j] = value.astype(B16)
            if j < 3:
                self.direct.append(
                    self.send(self.acc.at[j], self.r3.at[j], self.s2.at[j], self.v2.at[j], self.second[j])
                )

    def step5(self):
        value = self.acc[3].astype(F32)
        for j in range(3):
            self.direct[j].wait_recv()
            value = value + self.r3[j].astype(F32)
        return value


def kernel(
    scale,
    x_hbm, w_hbm, enc_gain, enc_bias, mask_token, pos_hbm, dec_gains, head_hbm, head_bias, order, tgt_hbm,
    g_out, w_out,
    w, pos, head, tgt, lat, lat_in, dlat, dl_all,
    xb, pack, nq, rstd, acc, d_norm,
    stream, hidden, d_hidden, d_stream, tall, act, act_m, act_v, q, k, v, att, out_b, d_att, back, at, probs, wanted, err, gbuf,
    term, core_x, core_y, d1x, d1y, d2x, d2y, d3x, d3y, d4x, d4y, zr,
    term_e, e1, e2, e3, e4,
    w_sem, in_sem, out_sem, lat_send, lat_recv, dl_send, dl_recv, fw_send, fw_recv, nq_send, nq_recv,
    core_send, core_recv, s1, v1, s2, v2, zsend, zrecv,
):
    dp = lax.axis_index("dp")
    x = lax.axis_index("section")
    grp = lax.axis_index("grp")
    y = dp // 4
    z = (dp // 2) % 2
    c = dp % 2

    def at_y(t):
        return {"dp": t * 4 + z * 2 + c}

    def at_x(t):
        return {"section": t}

    to_core = {"dp": y * 4 + z * 2 + (1 - c)}
    to_z = {"dp": y * 4 + (1 - z) * 2 + c}
    to_grp = {"grp": 1 - grp}
    to_cross = {"grp": 1 - grp, "dp": y * 4 + (1 - z) * 2 + c}
    to_diag = {"dp": y * 4 + (1 - z) * 2 + (1 - c)}
    xs = [(x + 2) % 4, (x + 1) % 4, (x + 3) % 4, x]
    ys = [(y + 2) % 4, (y + 1) % 4, (y + 3) % 4, y]

    barrier = pltpu.get_barrier_semaphore()
    to_x = [at_x(xs[j]) for j in range(3)]
    to_y = [at_y(ys[j]) for j in range(3)]
    for who in [to_grp, to_cross, to_core, to_z, to_diag] + to_x + to_y:
        pl.semaphore_signal(barrier, inc=1, device_id=who, device_id_type=MESH)

    def remote(src, dst, send, recv, who):
        return pltpu.make_async_remote_copy(
            src_ref=src, dst_ref=dst, send_sem=send, recv_sem=recv, device_id=who, device_id_type=MESH
        )

    def sender(started):
        def send(src, dst, send_s, recv_s, who):
            copy = remote(src, dst, send_s, recv_s, who)
            copy.start()
            started.append(copy)
            return copy

        return send

    def w_copy(i):
        rows = pl.ds(pl.multiple_of(i * 512, 512), 512)
        return pltpu.make_async_copy(w_hbm.at[rows], w.at[rows], w_sem.at[i])

    x_copy = pltpu.make_async_copy(x_hbm, xb, in_sem.at[0])
    pos_copy = pltpu.make_async_copy(pos_hbm, pos, in_sem.at[1])
    head_copy = pltpu.make_async_copy(head_hbm, head, in_sem.at[2])
    tgt_copy = pltpu.make_async_copy(tgt_hbm, tgt, in_sem.at[3])
    lat_copy = remote(lat, lat_in, lat_send.at[0], lat_recv.at[0], to_grp)
    g_copy = pltpu.make_async_copy(gbuf, g_out, out_sem.at[0])

    @pl.when(grp == 0)
    def _():
        x_copy.start()

    @pl.when(grp == 1)
    def _():
        pos_copy.start()

    for i in range(8):
        w_copy(i).start()

    @pl.when(grp == 0)
    def _():
        x_copy.wait()
        squares = jnp.zeros((2 * VIS, 128), F32)
        for j in range(DE // 128):
            part = xb[:, j * 128 : (j + 1) * 128].astype(F32)
            squares = squares + part * part
        rs = lax.rsqrt(jnp.sum(squares, axis=-1, keepdims=True) * (1.0 / DE) + EPS)
        rstd[...] = jnp.broadcast_to(rs, (2 * VIS, 128))
        acc[...] = jnp.broadcast_to(enc_bias[...], (2 * VIS, D))

        def step(i):
            cols = span(i, 512)
            block = xb[:, cols].astype(F32) * rstd[:, 0:1] * enc_gain[:, cols]
            block = block.astype(B16)
            for j in range(2):
                pack[(i % 2) * 2 + j, :, span(i // 2, 256)] = block[:, j * 256 : (j + 1) * 256]
            w_copy(i).wait()
            acc[...] += nn(block, w[cols, :])

        loop(8, step, 8)
        lat[...] = acc[...].astype(B16)

    @pl.when(grp == 1)
    def _():
        tgt_copy.start()
        head_copy.start()
        pos_copy.wait()

        hi = pos[...].astype(B16)
        rest = pos[...] - hi.astype(F32)
        mid = rest.astype(B16)
        low = (rest - mid.astype(F32)).astype(B16)
        gain = dec_gains[0:1, :]
        hots = []
        for s in range(2):
            rows = lax.broadcasted_iota(jnp.int32, (L, L), 0)
            hot = jnp.where(rows == order[s, 0:1, :], 1.0, 0.0).T.astype(B16)
            hots.append(hot)
            found = (nn(hot, hi) + nn(hot, mid)) + nn(hot, low)
            stream[s * L : s * L + VIS, :] = found[:VIS]
            value = found[VIS:] + mask_token[...]
            stream[s * L + VIS : (s + 1) * L, :] = value
            normal = norm_rows(value, gain).astype(B16)
            act[s * L + VIS : (s + 1) * L, :] = normal
            act_m[s * (L - VIS) : (s + 1) * (L - VIS), :] = normal
        for part, dst in enumerate((q, k, v)):
            w_copy(2 * part).wait()
            w_copy(2 * part + 1).wait()
            value = nn(act_m[...], w[part * D : (part + 1) * D, :]).astype(B16)
            dst[VIS:L, :] = value[: L - VIS]
            dst[L + VIS :, :] = value[L - VIS :]
        tgt_copy.wait()
        for s in range(2):
            wanted[s * L : (s + 1) * L, :] = nn(hots[s], tgt[s]).astype(B16)
        for i in range(6, 8):
            w_copy(i).wait()
        head_copy.wait()

    pl.semaphore_wait(barrier, 11)

    @pl.when(grp == 0)
    def _():
        lat_copy.start()
        lat_copy.wait_send()
        me = z * 2 + c
        nq[me] = pack[me]
        copies = []
        for j, (place, who) in enumerate(((z * 2 + 1 - c, to_core), ((1 - z) * 2 + c, to_z), ((1 - z) * 2 + 1 - c, to_diag))):
            copies.append(remote(pack.at[place], nq.at[me], nq_send.at[j], nq_recv.at[j], who))
            copies[-1].start()
        for copy in copies:
            copy.wait()
        at[0] = nq[...].reshape(4 * 2 * VIS, D).T

    @pl.when(grp == 1)
    def _():
        lat_copy.wait_recv()
        gain = dec_gains[0:1, :]
        for s in range(2):
            rows = slice(s * L, s * L + VIS)
            value = stream[rows, :] + lat_in[s * VIS : (s + 1) * VIS, :].astype(F32)
            stream[rows, :] = value
            normal = norm_rows(value, gain).astype(B16)
            act[rows, :] = normal
            act_v[s * VIS : (s + 1) * VIS, :] = normal
        for part, dst in enumerate((q, k, v)):
            value = nn(act_v[...], w[part * D : (part + 1) * D, :]).astype(B16)
            dst[:VIS, :] = value[:VIS]
            dst[L : L + VIS, :] = value[VIS:]

        shrink = 1.0 / math.sqrt(HS)

        def attend(i):
            rows = span(i // 4, L)
            cols = span(i % 4, GROUP)
            scores = nt(stack_heads(q[rows, cols]), k[rows, cols]) * shrink
            expo = jnp.exp(scores - jnp.max(scores, axis=-1, keepdims=True))
            p = expo * (1.0 / jnp.sum(expo, axis=-1, keepdims=True))
            probs[i] = p
            att[rows, cols] = fold_heads(nn(p.astype(B16), v[rows, cols])).astype(B16)

        loop(8, attend, 8)

        hidden[...] = stream[...] + nn(att[...], w[3 * D :, :])
        gain_out = dec_gains[1:2, :]

        def head_both(i):
            rows = span(i, L)
            out_b[rows, :] = norm_rows(hidden[rows, :], gain_out).astype(B16)
            pred = nn(out_b[rows, :], head[...]) + head_bias[...]
            err[rows, :] = (pred - wanted[rows, :].astype(F32)).astype(B16)
            value = norm_rows_back(hidden[rows, :], gain_out, nt(err[rows, :], head[...]))
            d_hidden[rows, :] = value
            back[3, rows, :] = value.astype(B16)

        loop(2, head_both, 2)
        d_att[...] = nt(back[3], w[3 * D :, :]).astype(B16)

        def attend_back(i):
            rows = span(i // 4, L)
            cols = span(i % 4, GROUP)
            p = probs[i]
            up = stack_heads(d_att[rows, cols])
            d_p = nt(up, v[rows, cols])
            d_s = p * (d_p - jnp.sum(d_p * p, axis=-1, keepdims=True)) * shrink
            d_s = d_s.astype(B16)
            back[2, rows, cols] = tn(p.astype(B16), up).astype(B16)
            back[0, rows, cols] = fold_heads(nn(d_s, k[rows, cols])).astype(B16)
            back[1, rows, cols] = tn(d_s, stack_heads(q[rows, cols])).astype(B16)

        loop(8, attend_back, 8)

        def act_back(part_of):
            total = nt(part_of(0), w[:D, :])
            total = total + nt(part_of(1), w[D : 2 * D, :])
            return total + nt(part_of(2), w[2 * D : 3 * D, :])

        def both(ref):
            return jnp.concatenate([ref[:VIS, :], ref[L : L + VIS, :]], 0)

        def keep(start, value):
            rows = value.shape[0]
            for t in range(8):
                tall[t, start : start + rows, :] = value[:, t * 128 : (t + 1) * 128]

        upstream = act_back(lambda part: both(back.at[part]))
        for s in range(2):
            rows = slice(s * L, s * L + VIS)
            value = d_hidden[rows, :] + norm_rows_back(stream[rows, :], gain, upstream[s * VIS : (s + 1) * VIS])
            keep(s * L, value)
            dlat[s * VIS : (s + 1) * VIS, :] = value.astype(B16)
        slot = dl_all.at[z * 2 + c]
        d_copies = [
            remote(dlat, slot, dl_send.at[0], dl_recv.at[z], to_grp),
            remote(dlat, slot, dl_send.at[1], dl_recv.at[z], to_cross),
        ]
        for copy in d_copies:
            copy.start()
        at[0] = act[...].T
        at[1] = att[...].T

        def masked_rows():
            for s in range(2):
                d_stream[s * L + VIS : (s + 1) * L, :] = act_back(lambda part: back[part, s * L + VIS : (s + 1) * L, :])
                for i in range(1, 4):
                    rows = slice(s * L + i * VIS, s * L + (i + 1) * VIS)
                    value = d_hidden[rows, :] + norm_rows_back(stream[rows, :], gain, d_stream[rows, :])
                    keep(s * L + i * VIS, value)
            for s in range(2):
                for j in range(4):
                    for t in range(8):
                        start = j * D + t * 128
                        gbuf[s, :, start : start + 128] = tall[t, pl.ds(s * L + j, VIS, stride=4), :].astype(B16)
            g_copy.start()

        started = []
        send = sender(started)

        def px(g, core, j):
            return term.at[g, :, :, core, j, pl.ds(0, 32)]

        def py(g, core, j):
            return term.at[g, j, :, core, :, pl.ds(32, 32)]

        def make(g):
            sems = lambda a: (s1.at[g, a], v1.at[g, a], s2.at[g, a], v2.at[g, a])
            return (
                Chunk(
                    lambda j: px(g, c, xs[j]), lambda ref, j: ref[ys[j]],
                    d1x.at[g], d2x.at[g], d3x.at[g], d4x.at[g], sems(0), to_x, to_y, send,
                ),
                Chunk(
                    lambda j: py(g, c, ys[j]), lambda ref, j: ref[:, xs[j]],
                    d1y.at[g], d2y.at[g], d3y.at[g], d4y.at[g], sems(1), to_y, to_x, send,
                ),
            )

        chunks = [make(g) for g in range(4)]
        cores, zs = {}, {}

        def stage(k, g):
            if k == 0:
                for blk in range(4):
                    value = nn(at[blk // 3], back[blk, :, g * 256 : (g + 1) * 256])
                    term[g, blk] = value.astype(B16).reshape(2, 2, 4, 64, 256)
                whole = term.at[g, :, :, 1 - c]
                cores[g, 0] = send(
                    whole.at[:, :, :, pl.ds(0, 32)], core_x.at[g], core_send.at[g, 0], core_recv.at[g, 0], to_core
                )
                cores[g, 1] = send(
                    whole.at[:, :, :, pl.ds(32, 32)], core_y.at[g], core_send.at[g, 1], core_recv.at[g, 1], to_core
                )
            if k == 1:
                for a in range(2):
                    cores[g, a].wait_recv()
                    got = (core_x, core_y)[a].at[g]
                    for j in range(4):
                        mine = chunks[g][a].view(j)
                        extra = got[:, :, xs[j]] if a == 0 else got[ys[j]]
                        mine[...] = mine[...] + extra
                        if j == 0:
                            chunks[g][a].step1()
                        if j == 2:
                            chunks[g][a].step2()
            if k == 2:
                for a in range(2):
                    chunks[g][a].step3()
            if k == 3:
                for a in range(2):
                    chunks[g][a].step4()
            if k == 4:
                for a in range(2):
                    value = chunks[g][a].step5()
                    mine = chunks[g][a].acc.at[3]
                    mine[...] = value.astype(B16)
                    zs[g, a] = send(mine.at[1 - z], zr.at[g, a], zsend.at[g, a], zrecv.at[g, a], to_z)
            if k == 5:
                for a in range(2):
                    zs[g, a].wait_recv()
                    value = chunks[g][a].acc[3, z].astype(F32) + zr[g, a].astype(F32)
                    w_out[a * 32 : (a + 1) * 32, g * 256 : (g + 1) * 256] = value * scale

        for d in range(9):
            for g in range(4):
                if 0 <= d - g < 6:
                    stage(d - g, g)
            if d == 4:
                masked_rows()
        for copy in d_copies + started:
            copy.wait_send()

    @pl.when(grp == 0)
    def _():
        passed = []
        for zz in range(2):
            slot = dl_all.at[zz * 2 + c]
            remote(dlat, slot, dl_send.at[0], dl_recv.at[zz], to_grp).wait_recv()
            passed.append(remote(slot, slot, fw_send.at[zz], fw_recv.at[zz], to_core))
            passed[-1].start()
        for copy in passed:
            copy.wait_recv()
        started = []
        send = sender(started)

        def make(g):
            sems = lambda a: (s1.at[g, a], v1.at[g, a], s2.at[g, a], v2.at[g, a])
            return (
                Chunk(
                    lambda j: term_e.at[g, :, xs[j], pl.ds(0, 32)], lambda ref, j: ref[ys[j]],
                    e1.at[g, 0], e2.at[g, 0], e3.at[g, 0], e4.at[g, 0], sems(0), to_x, to_y, send,
                ),
                Chunk(
                    lambda j: term_e.at[g, ys[j], :, pl.ds(32, 32)], lambda ref, j: ref[xs[j]],
                    e1.at[g, 1], e2.at[g, 1], e3.at[g, 1], e4.at[g, 1], sems(1), to_y, to_x, send,
                ),
            )

        chunks = [make(g) for g in range(2)]
        for g in range(2):
            every = dl_all[:, :, g * 512 : (g + 1) * 512].reshape(4 * 2 * VIS, 512)
            term_e[g] = nn(at[0], every).astype(B16).reshape(4, 4, 64, 512)
            for a in range(2):
                chunks[g][a].step1()
                chunks[g][a].step2()

        own = dl_all[z * 2 + c]
        inner = jnp.zeros((2 * VIS, 1), F32)
        for i in range(4):
            cols = slice(i * D, (i + 1) * D)
            scaled = nt(own, w[cols, :]) * enc_gain[:, cols]
            d_norm[:, cols] = scaled
            inner = inner + jnp.sum(scaled * xb[:, cols].astype(F32), axis=-1, keepdims=True)
            if i == 1:
                for g in range(2):
                    for a in range(2):
                        chunks[g][a].step3()
        rs = rstd[:, 0:1]
        factor = rs * rs * rs * (inner * (1.0 / DE))
        for g in range(2):
            for a in range(2):
                chunks[g][a].step4()
        for i in range(8):
            cols = slice(i * 512, (i + 1) * 512)
            value = (rs * d_norm[:, cols] - xb[:, cols].astype(F32) * factor).astype(B16)
            gbuf[0, :, cols] = value[:VIS]
            gbuf[1, :, cols] = value[VIS:]
        g_copy.start()
        for g in range(2):
            for a in range(2):
                w_out[a * 32 : (a + 1) * 32, g * 512 : (g + 1) * 512] = chunks[g][a].step5() * scale
        for copy in passed + started:
            copy.wait_send()

    g_copy.wait()


def on_device(
    enc_input, weights, enc_gain, enc_bias, mask_token, pos_embed, dec_gains, head_weight, head_bias, order, targets
):
    V = pltpu.VMEM
    S = pltpu.SemaphoreType.DMA
    full = pl.BlockSpec(memory_space=pltpu.VMEM)
    hbm = pl.BlockSpec(memory_space=pl.ANY)
    count = 2 * lax.axis_size("dp") * lax.axis_size("section")
    grads, w_grad = pl.pallas_call(
        functools.partial(kernel, 1.0 / count),
        out_shape=(jax.ShapeDtypeStruct((2, VIS, DE), B16), jax.ShapeDtypeStruct((64, D), F32)),
        in_specs=[hbm, hbm, full, full, full, hbm, full, hbm, full, full, hbm],
        out_specs=(hbm, full),
        scratch_shapes=[
            V((DE, D), B16), V((L, D), F32), V((D, 256), B16), V((2, L, 256), B16),
            V((2 * VIS, D), B16), V((2 * VIS, D), B16), V((2 * VIS, D), B16), V((4, 2 * VIS, D), B16),
            V((2 * VIS, DE), B16), V((4, 2 * VIS, D), B16), V((4, 2 * VIS, D), B16), V((2 * VIS, 128), F32),
            V((2 * VIS, D), F32), V((2 * VIS, DE), F32),
            V((ROWS, D), F32), V((ROWS, D), F32), V((ROWS, D), F32), V((ROWS, D), F32), V((8, ROWS, 128), F32),
            V((ROWS, D), B16), V((ROWS - 2 * VIS, D), B16), V((2 * VIS, D), B16),
            V((ROWS, D), B16), V((ROWS, D), B16), V((ROWS, D), B16), V((ROWS, D), B16),
            V((ROWS, D), B16), V((ROWS, D), B16), V((4, ROWS, D), B16), V((2, D, ROWS), B16),
            V((8, HEADS * L, L), F32), V((ROWS, 256), B16), V((ROWS, 256), B16), V((2, VIS, DE), B16),
            V((4, 4, 2, 2, 4, 64, 256), B16),
            V((4, 4, 2, 4, 32, 256), B16), V((4, 4, 2, 4, 32, 256), B16),
            V((4, 2, 2, 2, 32, 256), B16), V((4, 2, 1, 4, 32, 256), B16),
            V((4, 2, 4, 2, 32, 256), B16), V((4, 2, 2, 4, 32, 256), B16),
            V((4, 4, 2, 32, 256), B16), V((4, 4, 2, 32, 256), B16),
            V((4, 3, 2, 32, 256), B16), V((4, 3, 2, 32, 256), B16),
            V((4, 2, 32, 256), B16),
            V((2, 4, 4, 64, 512), B16), V((2, 2, 2, 2, 32, 512), B16), V((2, 2, 2, 4, 32, 512), B16),
            V((2, 2, 4, 32, 512), B16), V((2, 2, 3, 32, 512), B16),
            S((8,)), S((4,)), S((1,)), S((1,)), S((1,)), S((2,)), S((2,)), S((2,)), S((2,)), S((3,)), S((3,)),
            S((4, 2)), S((4, 2)), S((4, 2, 6)), S((4, 2, 6)), S((4, 2, 3)), S((4, 2, 3)), S((4, 2)), S((4, 2)),
        ],
        compiler_params=pltpu.CompilerParams(
            collective_id=0, has_side_effects=True, vmem_limit_bytes=60 * 2**20
        ),
        name="window",
    )(
        enc_input.reshape(2 * VIS, DE), weights[0], enc_gain[None], enc_bias[None], mask_token[None], pos_embed,
        dec_gains, head_weight, head_bias[None], order, targets.reshape(2, L, 256),
    )
    return grads[None, :, None], w_grad[None]


def solution(mesh):
    many = ("dp", "section")
    in_specs = (
        P(None, many, None, None), P("grp", None, None), P(), P(), P(), P(), P(), P(), P(),
        P(None, many, None), P(None, many, None, None),
    )
    out_specs = (P("grp", None, many, None, None), P("grp", many, None))
    return jax.shard_map(on_device, mesh=mesh, in_specs=in_specs, out_specs=out_specs, check_vma=False)
```

```python
import functools
import math

import jax
import jax.numpy as jnp
from jax import lax
from jax.experimental import pallas as pl
from jax.experimental.pallas import tpu as pltpu
from jax.sharding import PartitionSpec as P

MESH = pl.DeviceIdType.MESH
B16 = jnp.bfloat16
F32 = jnp.float32
EPS = 1e-06
PLAN = (
    "b0", "00", "b1", "b2", "10", "b3", "v", "01", "20", "02",
    "11", "03", "12", "30", "13", "21", "m", "22", "31", "40",
    "23", "32", "41", "50", "33", "42", "51", "43", "52", "53",
)
D = 1024
DE = 4096
L = 192
VIS = 48
HS = 64
ROWS = 2 * L
GROUP = 256
HEADS = GROUP // HS
NT = (((1,), (1,)), ((), ()))
TN = (((0,), (0,)), ((), ()))


def nn(a, b):
    return jnp.dot(a, b, preferred_element_type=F32)


def nt(a, b):
    return lax.dot_general(a, b, NT, preferred_element_type=F32)


def tn(a, b):
    return lax.dot_general(a, b, TN, preferred_element_type=F32)


def loop(n, body, unroll=1):
    def step(i, carry):
        body(i)
        return carry

    lax.fori_loop(0, n, step, 0, unroll=unroll)


def span(i, size):
    return pl.ds(pl.multiple_of(i * size, size), size)


def head_mask(h):
    return lax.broadcasted_iota(jnp.int32, (L, GROUP), 1) // HS == h


def stack_heads(block):
    zero = jnp.zeros_like(block)
    return jnp.concatenate([jnp.where(head_mask(h), block, zero) for h in range(HEADS)], 0)


def fold_heads(block):
    out = jnp.where(head_mask(0), block[:L], 0.0)
    for h in range(1, HEADS):
        out = jnp.where(head_mask(h), block[h * L : (h + 1) * L], out)
    return out


def norm_rows(values, gain):
    rstd = lax.rsqrt(jnp.mean(values * values, axis=-1, keepdims=True) + EPS)
    return values * rstd * gain


def norm_rows_back(values, gain, upstream):
    rstd = lax.rsqrt(jnp.mean(values * values, axis=-1, keepdims=True) + EPS)
    scaled = upstream * gain
    inner = jnp.mean(scaled * values, axis=-1, keepdims=True)
    return rstd * scaled - values * (rstd * rstd * rstd) * inner


class Chunk:
    def __init__(self, view, pick, r1, r2, acc, r3, sems, first, second, send):
        self.view, self.pick, self.r1, self.r2, self.acc, self.r3 = view, pick, r1, r2, acc, r3
        self.s1, self.v1, self.s2, self.v2 = sems
        if isinstance(pick, tuple):
            self.pick_z, self.targets = pick
        self.first, self.second, self.send = first, second, send

    def half(self, ref, h):
        n = ref.shape[0] // 2
        return ref.at[pl.ds(h * n, n)]

    def go(self, src, dst, k, who):
        return self.send(src, dst, self.s1.at[k], self.v1.at[k], who)

    def step1(self):
        plus, minus = self.first[1:3]
        self.c0 = self.go(self.half(self.view(0), 0), self.r1.at[0], 0, plus)
        self.c1 = self.go(self.half(self.view(0), 1), self.r1.at[1], 1, minus)

    def step2(self):
        plus, minus = self.first[1:3]
        self.c2 = self.go(self.half(self.view(1), 1), self.half(self.r2.at[0], 1), 2, plus)
        self.c3 = self.go(self.half(self.view(2), 0), self.half(self.r2.at[1], 0), 3, minus)

    def step3(self):
        plus, minus = self.first[1:3]
        self.c0.wait_recv()
        mine = self.half(self.view(1), 0)
        mine[...] = mine[...] + self.r1[0]
        self.c4 = self.go(mine, self.half(self.r2.at[0], 0), 4, plus)
        self.c1.wait_recv()
        mine = self.half(self.view(2), 1)
        mine[...] = mine[...] + self.r1[1]
        self.c5 = self.go(mine, self.half(self.r2.at[1], 1), 5, minus)

    def step4(self):
        for copy in (self.c2, self.c3, self.c4, self.c5):
            copy.wait_recv()
        self.direct = []
        for j in range(4):
            value = self.pick(self.view(3), j).astype(F32)
            value = value + self.pick(self.r2.at[0], j).astype(F32) + self.pick(self.r2.at[1], j).astype(F32)
            self.acc[j] = value.astype(B16)
            if j < 3:
                self.direct.append(
                    self.send(self.acc.at[j], self.r3.at[j], self.s2.at[j], self.v2.at[j], self.second[j])
                )

    def cross(self, send_sem, recv_sem, to_z, z, zr):
        for copy in (self.c2, self.c3, self.c4, self.c5):
            copy.wait_recv()
        for j, zz in ((0, 1 - z), (1, z)):
            value = self.pick_z(self.view(3), zz).astype(F32)
            value = value + self.pick_z(self.r2.at[0], zz).astype(F32) + self.pick_z(self.r2.at[1], zz).astype(F32)
            self.acc[j] = value.astype(B16)
            if j == 0:
                self.zc = self.send(self.acc.at[0], zr, send_sem, recv_sem, to_z)

    def spread(self, zr):
        self.zc.wait_recv()
        self.direct = []
        self.acc[1] = self.acc[1] + zr[...]
        for j in range(3):
            self.direct.append(
                self.send(
                    self.acc.at[1, self.targets[j]], self.r3.at[j], self.s2.at[j], self.v2.at[j], self.second[j]
                )
            )

    def last(self):
        value = self.acc[1, self.targets[3]].astype(F32)
        for j in range(3):
            self.direct[j].wait_recv()
            value = value + self.r3[j].astype(F32)
        return value

    def step5(self):
        value = self.acc[3].astype(F32)
        for j in range(3):
            self.direct[j].wait_recv()
            value = value + self.r3[j].astype(F32)
        return value


def kernel(
    scale,
    x_hbm, w_hbm, enc_gain, enc_bias, mask_token, pos_hbm, dec_gains, head_hbm, head_bias, order, tgt_hbm,
    g_out, w_out,
    w, pos, head, tgt, lat, lat_in, dlat, dl_all,
    xb, pack, nq, rstd, acc, d_norm,
    stream, hidden, d_hidden, d_stream, tall, act, act_m, act_v, q, k, v, att, out_b, d_att, back, at, probs, wanted, err, gbuf,
    term, core_x, core_y, d1x, d1y, d2x, d2y, d3x, d3y, d4x, d4y, zr,
    term_e, e1, e2, e3, e4,
    w_sem, in_sem, out_sem, lat_send, lat_recv, dl_send, dl_recv, fw_send, fw_recv, nq_send, nq_recv,
    core_send, core_recv, s1, v1, s2, v2, zsend, zrecv,
):
    dp = lax.axis_index("dp")
    x = lax.axis_index("section")
    grp = lax.axis_index("grp")
    y = dp // 4
    z = (dp // 2) % 2
    c = dp % 2

    def at_y(t):
        return {"dp": t * 4 + z * 2 + c}

    def at_x(t):
        return {"section": t}

    to_core = {"dp": y * 4 + z * 2 + (1 - c)}
    to_z = {"dp": y * 4 + (1 - z) * 2 + c}
    to_grp = {"grp": 1 - grp}
    to_cross = {"grp": 1 - grp, "dp": y * 4 + (1 - z) * 2 + c}
    to_diag = {"dp": y * 4 + (1 - z) * 2 + (1 - c)}
    xs = [(x + 2) % 4, (x + 1) % 4, (x + 3) % 4, x]
    ys = [(y + 2) % 4, (y + 1) % 4, (y + 3) % 4, y]

    barrier = pltpu.get_barrier_semaphore()
    to_x = [at_x(xs[j]) for j in range(3)]
    to_y = [at_y(ys[j]) for j in range(3)]
    for who in [to_grp, to_cross, to_core, to_z, to_diag] + to_x + to_y:
        pl.semaphore_signal(barrier, inc=1, device_id=who, device_id_type=MESH)

    def remote(src, dst, send, recv, who):
        return pltpu.make_async_remote_copy(
            src_ref=src, dst_ref=dst, send_sem=send, recv_sem=recv, device_id=who, device_id_type=MESH
        )

    def sender(started):
        def send(src, dst, send_s, recv_s, who):
            copy = remote(src, dst, send_s, recv_s, who)
            copy.start()
            started.append(copy)
            return copy

        return send

    def w_copy(i):
        rows = pl.ds(pl.multiple_of(i * 512, 512), 512)
        return pltpu.make_async_copy(w_hbm.at[rows], w.at[rows], w_sem.at[i])

    x_copy = pltpu.make_async_copy(x_hbm, xb, in_sem.at[0])
    pos_copy = pltpu.make_async_copy(pos_hbm, pos, in_sem.at[1])
    head_copy = pltpu.make_async_copy(head_hbm, head, in_sem.at[2])
    tgt_copy = pltpu.make_async_copy(tgt_hbm, tgt, in_sem.at[3])
    lat_copy = remote(lat, lat_in, lat_send.at[0], lat_recv.at[0], to_grp)
    g_copy = pltpu.make_async_copy(gbuf, g_out, out_sem.at[0])

    @pl.when(grp == 0)
    def _():
        x_copy.start()

    @pl.when(grp == 1)
    def _():
        pos_copy.start()

    for i in range(8):
        w_copy(i).start()

    @pl.when(grp == 0)
    def _():
        x_copy.wait()
        squares = jnp.zeros((2 * VIS, 128), F32)
        for j in range(DE // 128):
            part = xb[:, j * 128 : (j + 1) * 128].astype(F32)
            squares = squares + part * part
        rs = lax.rsqrt(jnp.sum(squares, axis=-1, keepdims=True) * (1.0 / DE) + EPS)
        rstd[...] = jnp.broadcast_to(rs, (2 * VIS, 128))
        acc[...] = jnp.broadcast_to(enc_bias[...], (2 * VIS, D))

        def step(i):
            cols = span(i, 512)
            block = xb[:, cols].astype(F32) * rstd[:, 0:1] * enc_gain[:, cols]
            block = block.astype(B16)
            for j in range(2):
                pack[(i % 2) * 2 + j, :, span(i // 2, 256)] = block[:, j * 256 : (j + 1) * 256]
            w_copy(i).wait()
            acc[...] += nn(block, w[cols, :])

        loop(8, step, 8)
        lat[...] = acc[...].astype(B16)

    @pl.when(grp == 1)
    def _():
        tgt_copy.start()
        head_copy.start()
        pos_copy.wait()

        hi = pos[...].astype(B16)
        rest = pos[...] - hi.astype(F32)
        mid = rest.astype(B16)
        low = (rest - mid.astype(F32)).astype(B16)
        gain = dec_gains[0:1, :]
        hots = []
        for s in range(2):
            rows = lax.broadcasted_iota(jnp.int32, (L, L), 0)
            hot = jnp.where(rows == order[s, 0:1, :], 1.0, 0.0).T.astype(B16)
            hots.append(hot)
            found = (nn(hot, hi) + nn(hot, mid)) + nn(hot, low)
            stream[s * L : s * L + VIS, :] = found[:VIS]
            value = found[VIS:] + mask_token[...]
            stream[s * L + VIS : (s + 1) * L, :] = value
            normal = norm_rows(value, gain).astype(B16)
            act[s * L + VIS : (s + 1) * L, :] = normal
            act_m[s * (L - VIS) : (s + 1) * (L - VIS), :] = normal
        for part, dst in enumerate((q, k, v)):
            w_copy(2 * part).wait()
            w_copy(2 * part + 1).wait()
            value = nn(act_m[...], w[part * D : (part + 1) * D, :]).astype(B16)
            dst[VIS:L, :] = value[: L - VIS]
            dst[L + VIS :, :] = value[L - VIS :]
        tgt_copy.wait()
        for s in range(2):
            wanted[s * L : (s + 1) * L, :] = nn(hots[s], tgt[s]).astype(B16)
        for i in range(6, 8):
            w_copy(i).wait()
        head_copy.wait()

    pl.semaphore_wait(barrier, 11)

    @pl.when(grp == 0)
    def _():
        lat_copy.start()
        lat_copy.wait_send()
        me = z * 2 + c
        nq[me] = pack[me]
        copies = []
        for j, (place, who) in enumerate(((z * 2 + 1 - c, to_core), ((1 - z) * 2 + c, to_z), ((1 - z) * 2 + 1 - c, to_diag))):
            copies.append(remote(pack.at[place], nq.at[me], nq_send.at[j], nq_recv.at[j], who))
            copies[-1].start()
        for copy in copies:
            copy.wait()
        at[0] = nq[...].reshape(4 * 2 * VIS, D).T

    @pl.when(grp == 1)
    def _():
        lat_copy.wait_recv()
        gain = dec_gains[0:1, :]
        for s in range(2):
            rows = slice(s * L, s * L + VIS)
            value = stream[rows, :] + lat_in[s * VIS : (s + 1) * VIS, :].astype(F32)
            stream[rows, :] = value
            normal = norm_rows(value, gain).astype(B16)
            act[rows, :] = normal
            act_v[s * VIS : (s + 1) * VIS, :] = normal
        for part, dst in enumerate((q, k, v)):
            value = nn(act_v[...], w[part * D : (part + 1) * D, :]).astype(B16)
            dst[:VIS, :] = value[:VIS]
            dst[L : L + VIS, :] = value[VIS:]

        shrink = 1.0 / math.sqrt(HS)

        def attend(i):
            rows = span(i // 4, L)
            cols = span(i % 4, GROUP)
            scores = nt(stack_heads(q[rows, cols]), k[rows, cols]) * shrink
            expo = jnp.exp(scores - jnp.max(scores, axis=-1, keepdims=True))
            p = expo * (1.0 / jnp.sum(expo, axis=-1, keepdims=True))
            probs[i] = p
            att[rows, cols] = fold_heads(nn(p.astype(B16), v[rows, cols])).astype(B16)

        loop(8, attend, 8)

        hidden[...] = stream[...] + nn(att[...], w[3 * D :, :])
        gain_out = dec_gains[1:2, :]

        def head_both(i):
            rows = span(i, L)
            out_b[rows, :] = norm_rows(hidden[rows, :], gain_out).astype(B16)
            pred = nn(out_b[rows, :], head[...]) + head_bias[...]
            err[rows, :] = (pred - wanted[rows, :].astype(F32)).astype(B16)
            value = norm_rows_back(hidden[rows, :], gain_out, nt(err[rows, :], head[...]))
            d_hidden[rows, :] = value
            back[3, rows, :] = value.astype(B16)

        loop(2, head_both, 2)
        d_att[...] = nt(back[3], w[3 * D :, :]).astype(B16)

        at[0] = act[...].T
        at[1] = att[...].T

        def attend_back(g):
            cols = slice(g * GROUP, (g + 1) * GROUP)
            for s in range(2):
                rows = slice(s * L, (s + 1) * L)
                p = probs[s * 4 + g]
                up = stack_heads(d_att[rows, cols])
                d_p = nt(up, v[rows, cols])
                d_s = p * (d_p - jnp.sum(d_p * p, axis=-1, keepdims=True)) * shrink
                d_s = d_s.astype(B16)
                back[2, rows, cols] = tn(p.astype(B16), up).astype(B16)
                back[0, rows, cols] = fold_heads(nn(d_s, k[rows, cols])).astype(B16)
                back[1, rows, cols] = tn(d_s, stack_heads(q[rows, cols])).astype(B16)

        def act_back(part_of):
            total = nt(part_of(0), w[:D, :])
            total = total + nt(part_of(1), w[D : 2 * D, :])
            return total + nt(part_of(2), w[2 * D : 3 * D, :])

        def both(ref):
            return jnp.concatenate([ref[:VIS, :], ref[L : L + VIS, :]], 0)

        def keep(start, value):
            rows = value.shape[0]
            for t in range(8):
                tall[t, start : start + rows, :] = value[:, t * 128 : (t + 1) * 128]

        def visible_rows():
            upstream = act_back(lambda part: both(back.at[part]))
            for s in range(2):
                rows = slice(s * L, s * L + VIS)
                value = d_hidden[rows, :] + norm_rows_back(stream[rows, :], gain, upstream[s * VIS : (s + 1) * VIS])
                keep(s * L, value)
                dlat[s * VIS : (s + 1) * VIS, :] = value.astype(B16)
            slot = dl_all.at[z * 2 + c]
            d_copies = [
                remote(dlat, slot, dl_send.at[0], dl_recv.at[z], to_grp),
                remote(dlat, slot, dl_send.at[1], dl_recv.at[z], to_cross),
            ]
            for copy in d_copies:
                copy.start()
            return d_copies

        def masked_rows():
            for s in range(2):
                d_stream[s * L + VIS : (s + 1) * L, :] = act_back(lambda part: back[part, s * L + VIS : (s + 1) * L, :])
                for i in range(1, 4):
                    rows = slice(s * L + i * VIS, s * L + (i + 1) * VIS)
                    value = d_hidden[rows, :] + norm_rows_back(stream[rows, :], gain, d_stream[rows, :])
                    keep(s * L + i * VIS, value)
            for s in range(2):
                for j in range(4):
                    for t in range(8):
                        start = j * D + t * 128
                        gbuf[s, :, start : start + 128] = tall[t, pl.ds(s * L + j, VIS, stride=4), :].astype(B16)
            g_copy.start()

        started = []
        send = sender(started)

        def px(g, core, j):
            return term.at[g, :, :, core, j, pl.ds(0, 32)]

        def py(g, core, j):
            return term.at[g, j, :, core, :, pl.ds(32, 32)]

        def make(g):
            sems = lambda a: (s1.at[g, a], v1.at[g, a], s2.at[g, a], v2.at[g, a])
            return (
                Chunk(
                    lambda j: px(g, c, xs[j]), (lambda ref, zz: ref[:, zz], ys),
                    d1x.at[g], d2x.at[g], d3x.at[g], d4x.at[g], sems(0), to_x, to_y, send,
                ),
                Chunk(
                    lambda j: py(g, c, ys[j]), (lambda ref, zz: ref[zz], xs),
                    d1y.at[g], d2y.at[g], d3y.at[g], d4y.at[g], sems(1), to_y, to_x, send,
                ),
            )

        chunks = [make(g) for g in range(4)]
        cores = {}

        def stage(k, g):
            if k == 0:
                for blk in range(4):
                    value = nn(at[blk // 3], back[blk, :, g * 256 : (g + 1) * 256])
                    term[g, blk] = value.astype(B16).reshape(2, 2, 4, 64, 256)
                whole = term.at[g, :, :, 1 - c]
                cores[g, 0] = send(
                    whole.at[:, :, :, pl.ds(0, 32)], core_x.at[g], core_send.at[g, 0], core_recv.at[g, 0], to_core
                )
                cores[g, 1] = send(
                    whole.at[:, :, :, pl.ds(32, 32)], core_y.at[g], core_send.at[g, 1], core_recv.at[g, 1], to_core
                )
            if k == 1:
                for a in range(2):
                    cores[g, a].wait_recv()
                    got = (core_x, core_y)[a].at[g]
                    for j in range(4):
                        mine = chunks[g][a].view(j)
                        extra = got[:, :, xs[j]] if a == 0 else got[ys[j]]
                        mine[...] = mine[...] + extra
                        if j == 0:
                            chunks[g][a].step1()
                        if j == 2:
                            chunks[g][a].step2()
            if k == 2:
                for a in range(2):
                    chunks[g][a].step3()
            if k == 3:
                for a in range(2):
                    chunks[g][a].cross(zsend.at[g, a], zrecv.at[g, a], to_z, z, zr.at[g, a])
            if k == 4:
                for a in range(2):
                    chunks[g][a].spread(zr.at[g, a])
            if k == 5:
                for a in range(2):
                    w_out[a * 32 : (a + 1) * 32, g * 256 : (g + 1) * 256] = chunks[g][a].last() * scale

        d_copies = []
        for word in PLAN:
            if word == "v":
                d_copies = visible_rows()
            elif word == "m":
                masked_rows()
            elif word[0] == "b":
                attend_back(int(word[1]))
            else:
                stage(int(word[0]), int(word[1]))
        for copy in d_copies + started:
            copy.wait_send()

    @pl.when(grp == 0)
    def _():
        passed = []
        for zz in range(2):
            slot = dl_all.at[zz * 2 + c]
            remote(dlat, slot, dl_send.at[0], dl_recv.at[zz], to_grp).wait_recv()
            passed.append(remote(slot, slot, fw_send.at[zz], fw_recv.at[zz], to_core))
            passed[-1].start()
        for copy in passed:
            copy.wait_recv()
        started = []
        send = sender(started)

        def make(g):
            sems = lambda a: (s1.at[g, a], v1.at[g, a], s2.at[g, a], v2.at[g, a])
            return (
                Chunk(
                    lambda j: term_e.at[g, :, xs[j], pl.ds(0, 32)], lambda ref, j: ref[ys[j]],
                    e1.at[g, 0], e2.at[g, 0], e3.at[g, 0], e4.at[g, 0], sems(0), to_x, to_y, send,
                ),
                Chunk(
                    lambda j: term_e.at[g, ys[j], :, pl.ds(32, 32)], lambda ref, j: ref[xs[j]],
                    e1.at[g, 1], e2.at[g, 1], e3.at[g, 1], e4.at[g, 1], sems(1), to_y, to_x, send,
                ),
            )

        chunks = [make(g) for g in range(2)]
        for g in range(2):
            every = dl_all[:, :, g * 512 : (g + 1) * 512].reshape(4 * 2 * VIS, 512)
            term_e[g] = nn(at[0], every).astype(B16).reshape(4, 4, 64, 512)
            for a in range(2):
                chunks[g][a].step1()
                chunks[g][a].step2()

        own = dl_all[z * 2 + c]
        inner = jnp.zeros((2 * VIS, 1), F32)
        for i in range(4):
            cols = slice(i * D, (i + 1) * D)
            scaled = nt(own, w[cols, :]) * enc_gain[:, cols]
            d_norm[:, cols] = scaled
            inner = inner + jnp.sum(scaled * xb[:, cols].astype(F32), axis=-1, keepdims=True)
            if i == 1:
                for g in range(2):
                    for a in range(2):
                        chunks[g][a].step3()
        rs = rstd[:, 0:1]
        factor = rs * rs * rs * (inner * (1.0 / DE))
        for g in range(2):
            for a in range(2):
                chunks[g][a].step4()
        for i in range(8):
            cols = slice(i * 512, (i + 1) * 512)
            value = (rs * d_norm[:, cols] - xb[:, cols].astype(F32) * factor).astype(B16)
            gbuf[0, :, cols] = value[:VIS]
            gbuf[1, :, cols] = value[VIS:]
        g_copy.start()
        for g in range(2):
            for a in range(2):
                w_out[a * 32 : (a + 1) * 32, g * 512 : (g + 1) * 512] = chunks[g][a].step5() * scale
        for copy in passed + started:
            copy.wait_send()

    g_copy.wait()


def on_device(
    enc_input, weights, enc_gain, enc_bias, mask_token, pos_embed, dec_gains, head_weight, head_bias, order, targets
):
    V = pltpu.VMEM
    S = pltpu.SemaphoreType.DMA
    full = pl.BlockSpec(memory_space=pltpu.VMEM)
    hbm = pl.BlockSpec(memory_space=pl.ANY)
    count = 2 * lax.axis_size("dp") * lax.axis_size("section")
    grads, w_grad = pl.pallas_call(
        functools.partial(kernel, 1.0 / count),
        out_shape=(jax.ShapeDtypeStruct((2, VIS, DE), B16), jax.ShapeDtypeStruct((64, D), F32)),
        in_specs=[hbm, hbm, full, full, full, hbm, full, hbm, full, full, hbm],
        out_specs=(hbm, full),
        scratch_shapes=[
            V((DE, D), B16), V((L, D), F32), V((D, 256), B16), V((2, L, 256), B16),
            V((2 * VIS, D), B16), V((2 * VIS, D), B16), V((2 * VIS, D), B16), V((4, 2 * VIS, D), B16),
            V((2 * VIS, DE), B16), V((4, 2 * VIS, D), B16), V((4, 2 * VIS, D), B16), V((2 * VIS, 128), F32),
            V((2 * VIS, D), F32), V((2 * VIS, DE), F32),
            V((ROWS, D), F32), V((ROWS, D), F32), V((ROWS, D), F32), V((ROWS, D), F32), V((8, ROWS, 128), F32),
            V((ROWS, D), B16), V((ROWS - 2 * VIS, D), B16), V((2 * VIS, D), B16),
            V((ROWS, D), B16), V((ROWS, D), B16), V((ROWS, D), B16), V((ROWS, D), B16),
            V((ROWS, D), B16), V((ROWS, D), B16), V((4, ROWS, D), B16), V((2, D, ROWS), B16),
            V((8, HEADS * L, L), F32), V((ROWS, 256), B16), V((ROWS, 256), B16), V((2, VIS, DE), B16),
            V((4, 4, 2, 2, 4, 64, 256), B16),
            V((4, 4, 2, 4, 32, 256), B16), V((4, 4, 2, 4, 32, 256), B16),
            V((4, 2, 2, 2, 32, 256), B16), V((4, 2, 1, 4, 32, 256), B16),
            V((4, 2, 4, 2, 32, 256), B16), V((4, 2, 2, 4, 32, 256), B16),
            V((4, 2, 4, 32, 256), B16), V((4, 2, 4, 32, 256), B16),
            V((4, 3, 32, 256), B16), V((4, 3, 32, 256), B16),
            V((4, 2, 4, 32, 256), B16),
            V((2, 4, 4, 64, 512), B16), V((2, 2, 2, 2, 32, 512), B16), V((2, 2, 2, 4, 32, 512), B16),
            V((2, 2, 4, 32, 512), B16), V((2, 2, 3, 32, 512), B16),
            S((8,)), S((4,)), S((1,)), S((1,)), S((1,)), S((2,)), S((2,)), S((2,)), S((2,)), S((3,)), S((3,)),
            S((4, 2)), S((4, 2)), S((4, 2, 6)), S((4, 2, 6)), S((4, 2, 3)), S((4, 2, 3)), S((4, 2)), S((4, 2)),
        ],
        compiler_params=pltpu.CompilerParams(
            collective_id=0, has_side_effects=True, vmem_limit_bytes=60 * 2**20
        ),
        name="window",
    )(
        enc_input.reshape(2 * VIS, DE), weights[0], enc_gain[None], enc_bias[None], mask_token[None], pos_embed,
        dec_gains, head_weight, head_bias[None], order, targets.reshape(2, L, 256),
    )

    def deliver(a_in, b_in, a_out, b_out, a_mid, b_mid, sem):
        steps = []
        for i in range(2):
            steps.append((a_in.at[i], a_mid.at[i], a_out.at[i], sem.at[i]))
        steps.append((b_in, b_mid, b_out, sem.at[2]))
        for src, mid, _, one in steps:
            pltpu.make_async_copy(src, mid, one).start()
        for src, mid, dst, one in steps:
            pltpu.make_async_copy(src, mid, one).wait()
            pltpu.make_async_copy(mid, dst, one).start()
        for _, mid, dst, one in steps:
            pltpu.make_async_copy(mid, dst, one).wait()

    grads, w_grad = pl.pallas_call(
        deliver,
        out_shape=(jax.ShapeDtypeStruct((2, VIS, DE), B16), jax.ShapeDtypeStruct((64, D), F32)),
        in_specs=[hbm, hbm],
        out_specs=(hbm, hbm),
        scratch_shapes=[V((2, VIS, DE), B16), V((64, D), F32), S((3,))],
        name="deliver",
    )(grads, w_grad)
    return grads[None, :, None], w_grad[None]


def solution(mesh):
    many = ("dp", "section")
    in_specs = (
        P(None, many, None, None), P("grp", None, None), P(), P(), P(), P(), P(), P(), P(),
        P(None, many, None), P(None, many, None, None),
    )
    out_specs = (P("grp", None, many, None, None), P("grp", many, None))
    return jax.shard_map(on_device, mesh=mesh, in_specs=in_specs, out_specs=out_specs, check_vma=False)
```

```python
import functools
import math

import jax
import jax.numpy as jnp
from jax import lax
from jax.experimental import pallas as pl
from jax.experimental.pallas import tpu as pltpu
from jax.sharding import PartitionSpec as P

MESH = pl.DeviceIdType.MESH
B16 = jnp.bfloat16
F32 = jnp.float32
EPS = 1e-06
PLAN = (
    "b0", "00", "b1", "b2", "b3", "10", "v", "01", "20", "02",
    "11", "03", "12", "30", "13", "21", "m", "22", "31", "40",
    "23", "32", "41", "50", "33", "42", "51", "43", "52", "53",
)
D = 1024
DE = 4096
L = 192
VIS = 48
HS = 64
ROWS = 2 * L
GROUP = 256
HEADS = GROUP // HS
NT = (((1,), (1,)), ((), ()))
TN = (((0,), (0,)), ((), ()))


def nn(a, b):
    return jnp.dot(a, b, preferred_element_type=F32)


def nt(a, b):
    return lax.dot_general(a, b, NT, preferred_element_type=F32)


def tn(a, b):
    return lax.dot_general(a, b, TN, preferred_element_type=F32)


def loop(n, body, unroll=1):
    def step(i, carry):
        body(i)
        return carry

    lax.fori_loop(0, n, step, 0, unroll=unroll)


def span(i, size):
    return pl.ds(pl.multiple_of(i * size, size), size)


def head_mask(h):
    return lax.broadcasted_iota(jnp.int32, (L, GROUP), 1) // HS == h


def stack_heads(block):
    zero = jnp.zeros_like(block)
    return jnp.concatenate([jnp.where(head_mask(h), block, zero) for h in range(HEADS)], 0)


def fold_heads(block):
    out = jnp.where(head_mask(0), block[:L], 0.0)
    for h in range(1, HEADS):
        out = jnp.where(head_mask(h), block[h * L : (h + 1) * L], out)
    return out


def norm_rows(values, gain):
    rstd = lax.rsqrt(jnp.mean(values * values, axis=-1, keepdims=True) + EPS)
    return values * rstd * gain


def norm_rows_back(values, gain, upstream):
    rstd = lax.rsqrt(jnp.mean(values * values, axis=-1, keepdims=True) + EPS)
    scaled = upstream * gain
    inner = jnp.mean(scaled * values, axis=-1, keepdims=True)
    return rstd * scaled - values * (rstd * rstd * rstd) * inner


class Chunk:
    def __init__(self, view, pick, r1, r2, acc, r3, sems, first, second, send):
        self.view, self.pick, self.r1, self.r2, self.acc, self.r3 = view, pick, r1, r2, acc, r3
        self.s1, self.v1, self.s2, self.v2 = sems
        if isinstance(pick, tuple):
            self.pick_z, self.targets = pick
        self.first, self.second, self.send = first, second, send

    def half(self, ref, h):
        n = ref.shape[0] // 2
        return ref.at[pl.ds(h * n, n)]

    def go(self, src, dst, k, who):
        return self.send(src, dst, self.s1.at[k], self.v1.at[k], who)

    def step1(self):
        plus, minus = self.first[1:3]
        self.c0 = self.go(self.half(self.view(0), 0), self.r1.at[0], 0, plus)
        self.c1 = self.go(self.half(self.view(0), 1), self.r1.at[1], 1, minus)

    def step2(self):
        plus, minus = self.first[1:3]
        self.c2 = self.go(self.half(self.view(1), 1), self.half(self.r2.at[0], 1), 2, plus)
        self.c3 = self.go(self.half(self.view(2), 0), self.half(self.r2.at[1], 0), 3, minus)

    def step3(self):
        plus, minus = self.first[1:3]
        self.c0.wait_recv()
        mine = self.half(self.view(1), 0)
        mine[...] = mine[...] + self.r1[0]
        self.c4 = self.go(mine, self.half(self.r2.at[0], 0), 4, plus)
        self.c1.wait_recv()
        mine = self.half(self.view(2), 1)
        mine[...] = mine[...] + self.r1[1]
        self.c5 = self.go(mine, self.half(self.r2.at[1], 1), 5, minus)

    def step4(self):
        for copy in (self.c2, self.c3, self.c4, self.c5):
            copy.wait_recv()
        self.direct = []
        for j in range(4):
            value = self.pick(self.view(3), j).astype(F32)
            value = value + self.pick(self.r2.at[0], j).astype(F32) + self.pick(self.r2.at[1], j).astype(F32)
            self.acc[j] = value.astype(B16)
            if j < 3:
                self.direct.append(
                    self.send(self.acc.at[j], self.r3.at[j], self.s2.at[j], self.v2.at[j], self.second[j])
                )

    def cross(self, send_sem, recv_sem, to_z, z, zr):
        for copy in (self.c2, self.c3, self.c4, self.c5):
            copy.wait_recv()
        for j, zz in ((0, 1 - z), (1, z)):
            value = self.pick_z(self.view(3), zz).astype(F32)
            value = value + self.pick_z(self.r2.at[0], zz).astype(F32) + self.pick_z(self.r2.at[1], zz).astype(F32)
            self.acc[j] = value.astype(B16)
            if j == 0:
                self.zc = self.send(self.acc.at[0], zr, send_sem, recv_sem, to_z)

    def spread(self, zr):
        self.zc.wait_recv()
        self.direct = []
        self.acc[1] = self.acc[1] + zr[...]
        for j in range(3):
            self.direct.append(
                self.send(
                    self.acc.at[1, self.targets[j]], self.r3.at[j], self.s2.at[j], self.v2.at[j], self.second[j]
                )
            )

    def last(self):
        value = self.acc[1, self.targets[3]].astype(F32)
        for j in range(3):
            self.direct[j].wait_recv()
            value = value + self.r3[j].astype(F32)
        return value

    def step5(self):
        value = self.acc[3].astype(F32)
        for j in range(3):
            self.direct[j].wait_recv()
            value = value + self.r3[j].astype(F32)
        return value


def kernel(
    scale,
    x_hbm, w_hbm, gain_hbm, bias_hbm, mask_hbm, pos_hbm, gains_hbm, head_hbm, hbias_hbm, order_hbm, tgt_hbm,
    g_out, w_out,
    w, pos, head, tgt, lat, lat_in, dlat, dl_all,
    xb, normed, pack, nq, rstd, d_norm,
    stream, hidden, d_hidden, d_stream, tall, act, act_m, act_v, q, k, v, att, out_b, d_att, back, at, probs, wanted, err, gbuf,
    term, core_x, core_y, d1x, d1y, d2x, d2y, d3x, d3y, d4x, d4y, zr,
    term_e, e1, e2, e3, e4,
    enc_gain, enc_bias, mask_token, dec_gains, head_bias, order, few_sem,
    w_sem, in_sem, out_sem, lat_send, lat_recv, dl_send, dl_recv, fw_send, fw_recv, nq_send, nq_recv,
    core_send, core_recv, s1, v1, s2, v2, zsend, zrecv,
):
    dp = lax.axis_index("dp")
    x = lax.axis_index("section")
    grp = lax.axis_index("grp")
    y = dp // 4
    z = (dp // 2) % 2
    c = dp % 2

    def at_y(t):
        return {"dp": t * 4 + z * 2 + c}

    def at_x(t):
        return {"section": t}

    to_core = {"dp": y * 4 + z * 2 + (1 - c)}
    to_z = {"dp": y * 4 + (1 - z) * 2 + c}
    to_grp = {"grp": 1 - grp}
    to_cross = {"grp": 1 - grp, "dp": y * 4 + (1 - z) * 2 + c}
    to_diag = {"dp": y * 4 + (1 - z) * 2 + (1 - c)}
    xs = [(x + 2) % 4, (x + 1) % 4, (x + 3) % 4, x]
    ys = [(y + 2) % 4, (y + 1) % 4, (y + 3) % 4, y]

    barrier = pltpu.get_barrier_semaphore()
    to_x = [at_x(xs[j]) for j in range(3)]
    to_y = [at_y(ys[j]) for j in range(3)]
    for who in [to_grp, to_cross, to_core, to_z, to_diag] + to_x + to_y:
        pl.semaphore_signal(barrier, inc=1, device_id=who, device_id_type=MESH)

    def remote(src, dst, send, recv, who):
        return pltpu.make_async_remote_copy(
            src_ref=src, dst_ref=dst, send_sem=send, recv_sem=recv, device_id=who, device_id_type=MESH
        )

    def sender(started):
        def send(src, dst, send_s, recv_s, who):
            copy = remote(src, dst, send_s, recv_s, who)
            copy.start()
            started.append(copy)
            return copy

        return send

    def w_copy(i):
        rows = pl.ds(pl.multiple_of(i * 512, 512), 512)
        return pltpu.make_async_copy(w_hbm.at[rows], w.at[rows], w_sem.at[i])

    few = [(gain_hbm, enc_gain), (bias_hbm, enc_bias), (mask_hbm, mask_token), (gains_hbm, dec_gains)]
    few += [(hbias_hbm, head_bias), (order_hbm, order)]
    few = [pltpu.make_async_copy(src, dst, few_sem.at[i]) for i, (src, dst) in enumerate(few)]
    x_copy = pltpu.make_async_copy(x_hbm, xb, in_sem.at[0])
    pos_copy = pltpu.make_async_copy(pos_hbm, pos, in_sem.at[1])
    head_copy = pltpu.make_async_copy(head_hbm, head, in_sem.at[2])
    tgt_copy = pltpu.make_async_copy(tgt_hbm, tgt, in_sem.at[3])
    lat_copies = [remote(lat.at[h], lat_in.at[h], lat_send.at[h], lat_recv.at[h], to_grp) for h in range(2)]

    def w_piece(h, i):
        part = (pl.ds(i * D, D), pl.ds(h * 512, 512))
        return pltpu.make_async_copy(w_hbm.at[part], w.at[part], w_sem.at[h * 4 + i])

    g_copy = pltpu.make_async_copy(gbuf, g_out, out_sem.at[0])

    @pl.when(grp == 0)
    def _():
        x_copy.start()
        for copy in few[:2]:
            copy.start()
        for h in range(2):
            for i in range(4):
                w_piece(h, i).start()

    @pl.when(grp == 1)
    def _():
        for copy in few[2:]:
            copy.start()
        pos_copy.start()
        for i in range(8):
            w_copy(i).start()

    def project_half(h):
        cols = slice(h * 512, (h + 1) * 512)
        total = jnp.broadcast_to(enc_bias[:, cols], (2 * VIS, 512))
        for i in range(4):
            w_piece(h, i).wait()
            rows = slice(i * D, (i + 1) * D)
            total = total + nn(normed[:, rows], w[rows, cols])
        lat[h] = total.astype(B16)

    @pl.when(grp == 0)
    def _():
        x_copy.wait()
        for copy in few[:2]:
            copy.wait()
        squares = jnp.zeros((2 * VIS, 128), F32)
        for j in range(DE // 128):
            part = xb[:, j * 128 : (j + 1) * 128].astype(F32)
            squares = squares + part * part
        rs = lax.rsqrt(jnp.sum(squares, axis=-1, keepdims=True) * (1.0 / DE) + EPS)
        rstd[...] = jnp.broadcast_to(rs, (2 * VIS, 128))

        def step(i):
            cols = span(i, 512)
            block = xb[:, cols].astype(F32) * rstd[:, 0:1] * enc_gain[:, cols]
            block = block.astype(B16)
            normed[:, cols] = block
            for j in range(2):
                pack[(i % 2) * 2 + j, :, span(i // 2, 256)] = block[:, j * 256 : (j + 1) * 256]

        loop(8, step, 8)
        project_half(0)

    @pl.when(grp == 1)
    def _():
        tgt_copy.start()
        head_copy.start()
        for copy in few[2:]:
            copy.wait()
        pos_copy.wait()

        hi = pos[...].astype(B16)
        rest = pos[...] - hi.astype(F32)
        mid = rest.astype(B16)
        low = (rest - mid.astype(F32)).astype(B16)
        gain = dec_gains[0:1, :]
        hots = []
        for s in range(2):
            rows = lax.broadcasted_iota(jnp.int32, (L, L), 0)
            hot = jnp.where(rows == order[s, 0:1, :], 1.0, 0.0).T.astype(B16)
            hots.append(hot)
            found = (nn(hot, hi) + nn(hot, mid)) + nn(hot, low)
            stream[s * L : s * L + VIS, :] = found[:VIS]
            value = found[VIS:] + mask_token[...]
            stream[s * L + VIS : (s + 1) * L, :] = value
            normal = norm_rows(value, gain).astype(B16)
            act[s * L + VIS : (s + 1) * L, :] = normal
            act_m[s * (L - VIS) : (s + 1) * (L - VIS), :] = normal
        for part, dst in enumerate((q, k, v)):
            w_copy(2 * part).wait()
            w_copy(2 * part + 1).wait()
            value = nn(act_m[...], w[part * D : (part + 1) * D, :]).astype(B16)
            dst[VIS:L, :] = value[: L - VIS]
            dst[L + VIS :, :] = value[L - VIS :]
        tgt_copy.wait()
        for s in range(2):
            wanted[s * L : (s + 1) * L, :] = nn(hots[s], tgt[s]).astype(B16)
        for i in range(6, 8):
            w_copy(i).wait()
        head_copy.wait()

    pl.semaphore_wait(barrier, 11)

    @pl.when(grp == 0)
    def _():
        lat_copies[0].start()
        project_half(1)
        lat_copies[1].start()
        for copy in lat_copies:
            copy.wait_send()
        me = z * 2 + c
        nq[me] = pack[me]
        copies = []
        for j, (place, who) in enumerate(((z * 2 + 1 - c, to_core), ((1 - z) * 2 + c, to_z), ((1 - z) * 2 + 1 - c, to_diag))):
            copies.append(remote(pack.at[place], nq.at[me], nq_send.at[j], nq_recv.at[j], who))
            copies[-1].start()
        for copy in copies:
            copy.wait()
        at[0] = nq[...].reshape(4 * 2 * VIS, D).T

    @pl.when(grp == 1)
    def _():
        for copy in lat_copies:
            copy.wait_recv()
        gain = dec_gains[0:1, :]
        for s in range(2):
            rows = slice(s * L, s * L + VIS)
            halves = [lat_in[h, s * VIS : (s + 1) * VIS, :] for h in range(2)]
            value = stream[rows, :] + jnp.concatenate(halves, 1).astype(F32)
            stream[rows, :] = value
            normal = norm_rows(value, gain).astype(B16)
            act[rows, :] = normal
            act_v[s * VIS : (s + 1) * VIS, :] = normal
        for part, dst in enumerate((q, k, v)):
            value = nn(act_v[...], w[part * D : (part + 1) * D, :]).astype(B16)
            dst[:VIS, :] = value[:VIS]
            dst[L : L + VIS, :] = value[VIS:]

        shrink = 1.0 / math.sqrt(HS)

        def attend(i):
            rows = span(i // 4, L)
            cols = span(i % 4, GROUP)
            scores = nt(stack_heads(q[rows, cols]), k[rows, cols]) * shrink
            expo = jnp.exp(scores - jnp.max(scores, axis=-1, keepdims=True))
            p = expo * (1.0 / jnp.sum(expo, axis=-1, keepdims=True))
            probs[i] = p
            att[rows, cols] = fold_heads(nn(p.astype(B16), v[rows, cols])).astype(B16)

        loop(8, attend, 8)

        hidden[...] = stream[...] + nn(att[...], w[3 * D :, :])
        gain_out = dec_gains[1:2, :]

        def head_both(i):
            rows = span(i, L)
            out_b[rows, :] = norm_rows(hidden[rows, :], gain_out).astype(B16)
            pred = nn(out_b[rows, :], head[...]) + head_bias[...]
            err[rows, :] = (pred - wanted[rows, :].astype(F32)).astype(B16)
            value = norm_rows_back(hidden[rows, :], gain_out, nt(err[rows, :], head[...]))
            d_hidden[rows, :] = value
            back[3, rows, :] = value.astype(B16)

        loop(2, head_both, 2)
        d_att[...] = nt(back[3], w[3 * D :, :]).astype(B16)

        at[0] = act[...].T
        at[1] = att[...].T

        def attend_back(g):
            cols = slice(g * GROUP, (g + 1) * GROUP)
            for s in range(2):
                rows = slice(s * L, (s + 1) * L)
                p = probs[s * 4 + g]
                up = stack_heads(d_att[rows, cols])
                d_p = nt(up, v[rows, cols])
                d_s = p * (d_p - jnp.sum(d_p * p, axis=-1, keepdims=True)) * shrink
                d_s = d_s.astype(B16)
                back[2, rows, cols] = tn(p.astype(B16), up).astype(B16)
                back[0, rows, cols] = fold_heads(nn(d_s, k[rows, cols])).astype(B16)
                back[1, rows, cols] = tn(d_s, stack_heads(q[rows, cols])).astype(B16)

        def act_back(part_of):
            total = nt(part_of(0), w[:D, :])
            total = total + nt(part_of(1), w[D : 2 * D, :])
            return total + nt(part_of(2), w[2 * D : 3 * D, :])

        def both(ref):
            return jnp.concatenate([ref[:VIS, :], ref[L : L + VIS, :]], 0)

        def keep(start, value):
            rows = value.shape[0]
            for t in range(8):
                tall[t, start : start + rows, :] = value[:, t * 128 : (t + 1) * 128]

        def visible_rows():
            upstream = act_back(lambda part: both(back.at[part]))
            for s in range(2):
                rows = slice(s * L, s * L + VIS)
                value = d_hidden[rows, :] + norm_rows_back(stream[rows, :], gain, upstream[s * VIS : (s + 1) * VIS])
                keep(s * L, value)
                dlat[s * VIS : (s + 1) * VIS, :] = value.astype(B16)
            slot = dl_all.at[z * 2 + c]
            d_copies = [
                remote(dlat, slot, dl_send.at[0], dl_recv.at[z], to_grp),
                remote(dlat, slot, dl_send.at[1], dl_recv.at[z], to_cross),
            ]
            for copy in d_copies:
                copy.start()
            return d_copies

        def masked_rows():
            for s in range(2):
                d_stream[s * L + VIS : (s + 1) * L, :] = act_back(lambda part: back[part, s * L + VIS : (s + 1) * L, :])
                for i in range(1, 4):
                    rows = slice(s * L + i * VIS, s * L + (i + 1) * VIS)
                    value = d_hidden[rows, :] + norm_rows_back(stream[rows, :], gain, d_stream[rows, :])
                    keep(s * L + i * VIS, value)
            for s in range(2):
                for j in range(4):
                    for t in range(8):
                        start = j * D + t * 128
                        gbuf[s, :, start : start + 128] = tall[t, pl.ds(s * L + j, VIS, stride=4), :].astype(B16)
            g_copy.start()

        started = []
        send = sender(started)

        def px(g, core, j):
            return term.at[g, :, :, core, j, pl.ds(0, 32)]

        def py(g, core, j):
            return term.at[g, j, :, core, :, pl.ds(32, 32)]

        def make(g):
            sems = lambda a: (s1.at[g, a], v1.at[g, a], s2.at[g, a], v2.at[g, a])
            return (
                Chunk(
                    lambda j: px(g, c, xs[j]), (lambda ref, zz: ref[:, zz], ys),
                    d1x.at[g], d2x.at[g], d3x.at[g], d4x.at[g], sems(0), to_x, to_y, send,
                ),
                Chunk(
                    lambda j: py(g, c, ys[j]), (lambda ref, zz: ref[zz], xs),
                    d1y.at[g], d2y.at[g], d3y.at[g], d4y.at[g], sems(1), to_y, to_x, send,
                ),
            )

        chunks = [make(g) for g in range(4)]
        cores = {}

        def stage(k, g):
            if k == 0:
                for blk in range(4):
                    value = nn(at[blk // 3], back[blk, :, g * 256 : (g + 1) * 256])
                    term[g, blk] = value.astype(B16).reshape(2, 2, 4, 64, 256)
                whole = term.at[g, :, :, 1 - c]
                cores[g, 0] = send(
                    whole.at[:, :, :, pl.ds(0, 32)], core_x.at[g], core_send.at[g, 0], core_recv.at[g, 0], to_core
                )
                cores[g, 1] = send(
                    whole.at[:, :, :, pl.ds(32, 32)], core_y.at[g], core_send.at[g, 1], core_recv.at[g, 1], to_core
                )
            if k == 1:
                for a in range(2):
                    cores[g, a].wait_recv()
                    got = (core_x, core_y)[a].at[g]
                    for j in range(4):
                        mine = chunks[g][a].view(j)
                        extra = got[:, :, xs[j]] if a == 0 else got[ys[j]]
                        mine[...] = mine[...] + extra
                        if j == 0:
                            chunks[g][a].step1()
                        if j == 2:
                            chunks[g][a].step2()
            if k == 2:
                for a in range(2):
                    chunks[g][a].step3()
            if k == 3:
                for a in range(2):
                    chunks[g][a].cross(zsend.at[g, a], zrecv.at[g, a], to_z, z, zr.at[g, a])
            if k == 4:
                for a in range(2):
                    chunks[g][a].spread(zr.at[g, a])
            if k == 5:
                for a in range(2):
                    w_out[a * 32 : (a + 1) * 32, g * 256 : (g + 1) * 256] = chunks[g][a].last() * scale

        d_copies = []
        for word in PLAN:
            if word == "v":
                d_copies = visible_rows()
            elif word == "m":
                masked_rows()
            elif word[0] == "b":
                attend_back(int(word[1]))
            else:
                stage(int(word[0]), int(word[1]))
        for copy in d_copies + started:
            copy.wait_send()

    @pl.when(grp == 0)
    def _():
        passed = []
        for zz in range(2):
            slot = dl_all.at[zz * 2 + c]
            remote(dlat, slot, dl_send.at[0], dl_recv.at[zz], to_grp).wait_recv()
            passed.append(remote(slot, slot, fw_send.at[zz], fw_recv.at[zz], to_core))
            passed[-1].start()
        for copy in passed:
            copy.wait_recv()
        started = []
        send = sender(started)

        def make(g):
            sems = lambda a: (s1.at[g, a], v1.at[g, a], s2.at[g, a], v2.at[g, a])
            return (
                Chunk(
                    lambda j: term_e.at[g, :, xs[j], pl.ds(0, 32)], lambda ref, j: ref[ys[j]],
                    e1.at[g, 0], e2.at[g, 0], e3.at[g, 0], e4.at[g, 0], sems(0), to_x, to_y, send,
                ),
                Chunk(
                    lambda j: term_e.at[g, ys[j], :, pl.ds(32, 32)], lambda ref, j: ref[xs[j]],
                    e1.at[g, 1], e2.at[g, 1], e3.at[g, 1], e4.at[g, 1], sems(1), to_y, to_x, send,
                ),
            )

        chunks = [make(g) for g in range(2)]
        for g in range(2):
            every = dl_all[:, :, g * 512 : (g + 1) * 512].reshape(4 * 2 * VIS, 512)
            term_e[g] = nn(at[0], every).astype(B16).reshape(4, 4, 64, 512)
            for a in range(2):
                chunks[g][a].step1()
                chunks[g][a].step2()

        own = dl_all[z * 2 + c]
        inner = jnp.zeros((2 * VIS, 1), F32)
        for i in range(4):
            cols = slice(i * D, (i + 1) * D)
            scaled = nt(own, w[cols, :]) * enc_gain[:, cols]
            d_norm[:, cols] = scaled
            inner = inner + jnp.sum(scaled * xb[:, cols].astype(F32), axis=-1, keepdims=True)
            if i == 1:
                for g in range(2):
                    for a in range(2):
                        chunks[g][a].step3()
        rs = rstd[:, 0:1]
        factor = rs * rs * rs * (inner * (1.0 / DE))
        for g in range(2):
            for a in range(2):
                chunks[g][a].step4()
        for i in range(8):
            cols = slice(i * 512, (i + 1) * 512)
            value = (rs * d_norm[:, cols] - xb[:, cols].astype(F32) * factor).astype(B16)
            gbuf[0, :, cols] = value[:VIS]
            gbuf[1, :, cols] = value[VIS:]
        g_copy.start()
        for g in range(2):
            for a in range(2):
                w_out[a * 32 : (a + 1) * 32, g * 512 : (g + 1) * 512] = chunks[g][a].step5() * scale
        for copy in passed + started:
            copy.wait_send()

    g_copy.wait()


def on_device(
    enc_input, weights, enc_gain, enc_bias, mask_token, pos_embed, dec_gains, head_weight, head_bias, order, targets
):
    V = pltpu.VMEM
    S = pltpu.SemaphoreType.DMA
    full = pl.BlockSpec(memory_space=pltpu.VMEM)
    hbm = pl.BlockSpec(memory_space=pl.ANY)
    count = 2 * lax.axis_size("dp") * lax.axis_size("section")
    grads, w_grad = pl.pallas_call(
        functools.partial(kernel, 1.0 / count),
        out_shape=(jax.ShapeDtypeStruct((2, VIS, DE), B16), jax.ShapeDtypeStruct((64, D), F32)),
        in_specs=[hbm] * 11,
        out_specs=(hbm, full),
        scratch_shapes=[
            V((DE, D), B16), V((L, D), F32), V((D, 256), B16), V((2, L, 256), B16),
            V((2, 2 * VIS, 512), B16), V((2, 2 * VIS, 512), B16), V((2 * VIS, D), B16), V((4, 2 * VIS, D), B16),
            V((2 * VIS, DE), B16), V((2 * VIS, DE), B16), V((4, 2 * VIS, D), B16), V((4, 2 * VIS, D), B16), V((2 * VIS, 128), F32),
            V((2 * VIS, DE), F32),
            V((ROWS, D), F32), V((ROWS, D), F32), V((ROWS, D), F32), V((ROWS, D), F32), V((8, ROWS, 128), F32),
            V((ROWS, D), B16), V((ROWS - 2 * VIS, D), B16), V((2 * VIS, D), B16),
            V((ROWS, D), B16), V((ROWS, D), B16), V((ROWS, D), B16), V((ROWS, D), B16),
            V((ROWS, D), B16), V((ROWS, D), B16), V((4, ROWS, D), B16), V((2, D, ROWS), B16),
            V((8, HEADS * L, L), F32), V((ROWS, 256), B16), V((ROWS, 256), B16), V((2, VIS, DE), B16),
            V((4, 4, 2, 2, 4, 64, 256), B16),
            V((4, 4, 2, 4, 32, 256), B16), V((4, 4, 2, 4, 32, 256), B16),
            V((4, 2, 2, 2, 32, 256), B16), V((4, 2, 1, 4, 32, 256), B16),
            V((4, 2, 4, 2, 32, 256), B16), V((4, 2, 2, 4, 32, 256), B16),
            V((4, 2, 4, 32, 256), B16), V((4, 2, 4, 32, 256), B16),
            V((4, 3, 32, 256), B16), V((4, 3, 32, 256), B16),
            V((4, 2, 4, 32, 256), B16),
            V((2, 4, 4, 64, 512), B16), V((2, 2, 2, 2, 32, 512), B16), V((2, 2, 2, 4, 32, 512), B16),
            V((2, 2, 4, 32, 512), B16), V((2, 2, 3, 32, 512), B16),
            V((1, DE), F32), V((1, D), F32), V((1, D), F32), V((2, D), F32), V((1, 256), F32), V((2, 1, L), jnp.int32), S((6,)),
            S((8,)), S((4,)), S((1,)), S((2,)), S((2,)), S((2,)), S((2,)), S((2,)), S((2,)), S((3,)), S((3,)),
            S((4, 2)), S((4, 2)), S((4, 2, 6)), S((4, 2, 6)), S((4, 2, 3)), S((4, 2, 3)), S((4, 2)), S((4, 2)),
        ],
        compiler_params=pltpu.CompilerParams(
            collective_id=0, has_side_effects=True, vmem_limit_bytes=60 * 2**20
        ),
        name="window",
    )(
        enc_input.reshape(2 * VIS, DE), weights[0], enc_gain[None], enc_bias[None], mask_token[None], pos_embed,
        dec_gains, head_weight, head_bias[None], order, targets.reshape(2, L, 256),
    )

    def deliver(a_in, b_in, a_out, b_out, a_mid, b_mid, sem):
        steps = []
        for i in range(2):
            steps.append((a_in.at[i], a_mid.at[i], a_out.at[i], sem.at[i]))
        steps.append((b_in, b_mid, b_out, sem.at[2]))
        for src, mid, _, one in steps:
            pltpu.make_async_copy(src, mid, one).start()
        for src, mid, dst, one in steps:
            pltpu.make_async_copy(src, mid, one).wait()
            pltpu.make_async_copy(mid, dst, one).start()
        for _, mid, dst, one in steps:
            pltpu.make_async_copy(mid, dst, one).wait()

    grads, w_grad = pl.pallas_call(
        deliver,
        out_shape=(jax.ShapeDtypeStruct((2, VIS, DE), B16), jax.ShapeDtypeStruct((64, D), F32)),
        in_specs=[hbm, hbm],
        out_specs=(hbm, hbm),
        scratch_shapes=[V((2, VIS, DE), B16), V((64, D), F32), S((3,))],
        name="deliver",
    )(grads, w_grad)
    return grads[None, :, None], w_grad[None]


def solution(mesh):
    many = ("dp", "section")
    in_specs = (
        P(None, many, None, None), P("grp", None, None), P(), P(), P(), P(), P(), P(), P(),
        P(None, many, None), P(None, many, None, None),
    )
    out_specs = (P("grp", None, many, None, None), P("grp", many, None))
    return jax.shard_map(on_device, mesh=mesh, in_specs=in_specs, out_specs=out_specs, check_vma=False)
```
